32 devices in a mesh: groups: 2 (over y), space: 4 (over z), probe: 4 (over x, core).
Axes of the slice: x: 2, y: 2, z: 4, core: 2. Of those that a mesh axis runs over, the one named last changes fastest.
Arguments:
- probe_amplitudes: float32 [8, 12, 64, 256], P(('groups', 'probe'), 'space'), parts along dimension 0, may hold values from -4 to 4
- site_mask: float32 [24, 64, 256], P(('groups', 'space')), parts along dimension 0, may hold values from 0 to 1, as said below
- couplings: float32 [3, 24, 64, 256], P(None, ('groups', 'space')), parts along dimension 1, may hold values from 0.3 to 1.5
- target: float32 [512], P('groups'), parts along dimension 0, may hold values from -3 to 3
Outputs:
- probe_costate: float32 [8, 12, 64, 256], P(('groups', 'probe'), 'space'), parts along dimension 0
- bond_grad: float32 [3, 24, 64, 256], P(None, ('groups', 'space'), 'probe'), parts along dimension 1
The draws below stay inside these ranges and needn't reach their ends.
There are 2 independent parts, one for each index of `groups`. The reference program is written for one: setup_inputs(seed, part) draws one part's arguments, and reference() takes and returns one part's arrays. A program takes and returns all parts, laid end to end along the dimension named above; each array names one. Nothing has to cross between parts.
Inputs may be any that keep to these rules, and one draw needn't show every extreme that they name: `site_mask`: 0 at a vacancy, at least 0.4 where a spin is present.
All inputs are finite; a program needn't handle non-finite values.
Results may differ from the reference program's by a relative error of at most 0.0003.
Values sent between devices are 32-bit elements; how exact they have to be, the bound alone decides.
A program may use at most 64 MiB of HBM per device.

```python
import jax
import jax.numpy as jnp
from jax import lax

NY = 64
NZ = 256
STEPS = 8
NW = 256
NX = 12
PROBES = 4


SCALE = 10.0


def occupancy_values(key):
    level = jax.random.randint(jax.random.fold_in(key, 11), (NX, NY, NZ), 0, 1000)
    weight = jax.random.uniform(jax.random.fold_in(key, 12), (NX, NY, NZ), jnp.float32, 0.4, 1.0)
    plane = jnp.arange(NX, dtype=jnp.int32)
    threshold = 300 + 600 * plane // NX
    return jnp.where(level < threshold[:, None, None], weight, jnp.zeros_like(weight))


def coupling_values(key, power):
    plane = (jnp.arange(NX, dtype=jnp.float32) + 0.5) / NX
    base = 0.45 + 0.9 * plane
    rough = jax.random.uniform(jax.random.fold_in(key, 23), (3, NX, NY, NZ), jnp.float32)
    factor = 0.7 + 0.4 * rough ** power
    return base[None, :, None, None] * factor


def probe_values(key):
    normal_draw = jax.random.normal(jax.random.fold_in(key, 31), (PROBES, NX, NY, NZ), jnp.float32)
    return jnp.clip(normal_draw, -4.0, 4.0)


def operate_drawn(vector, bonds):
    total = bonds[0] * (vector - jnp.roll(vector, -1, 0)) + jnp.roll(bonds[0], 1, 0) * (vector - jnp.roll(vector, 1, 0))
    for axis in (1, 2):
        total = total + bonds[axis] * (vector - jnp.roll(vector, -1, axis)) + jnp.roll(bonds[axis], 1, axis) * (vector - jnp.roll(vector, 1, axis))
    return total / SCALE - vector


def moment_values(present, couplings, probes):
    bonds = tuple((couplings[axis] * present * jnp.roll(present, -1, axis) for axis in range(3)))

    def single(amplitude):
        probe = amplitude * present
        earlier = probe
        current = operate_drawn(probe, bonds)
        totals = [jnp.sum(probe * earlier), jnp.sum(probe * current)]
        for step in range(1, STEPS):
            following = 2.0 * operate_drawn(current, bonds) - earlier
            earlier = current
            current = following
            totals.append(jnp.sum(probe * current))
        return jnp.stack(totals)
    return jnp.sum(lax.map(single, probes), 0) / (PROBES * NX * NY * NZ)


def model_spectrum(moments):
    count = STEPS + 1
    order = jnp.arange(count).astype(jnp.float32)
    theta = jnp.pi * (jnp.arange(NW).astype(jnp.float32) + 0.5) / NW
    table = jnp.cos(order[:, None] * theta[None, :])
    total = count + 1.0
    jackson = ((total - order) * jnp.cos(jnp.pi * order / total) + jnp.sin(jnp.pi * order / total) / jnp.tan(jnp.pi / total)) / total
    doubled = jnp.where(jnp.arange(count) > 0, 2.0, 1.0).astype(jnp.float32)
    return jnp.dot(doubled * jackson * moments, table, precision=lax.Precision.HIGHEST)


def draw_probe_amplitudes(key, part):
    return probe_values(key)


def draw_site_mask(key, part):
    return occupancy_values(key)


def draw_couplings(key, part):
    return coupling_values(key, 1.0)


def draw_target(key, part):
    present = occupancy_values(key)
    probes = probe_values(key)
    couplings = coupling_values(key, 1.0)
    moments = moment_values(present, couplings, probes)
    spectrum = model_spectrum(moments)
    key = jax.random.fold_in(key, 41)
    misfit = 0.05 * jax.random.normal(key, (NW,), jnp.float32)
    return jnp.clip(spectrum + misfit, -3.0, 3.0)


def setup_inputs(seed: int = 0, part: int = 0) -> dict:
    seeds = jax.random.split(jax.random.key(seed), 5)
    part_splits = jax.random.split(jax.random.fold_in(seeds[4], part), 5)
    probe_amplitudes = draw_probe_amplitudes(jax.random.fold_in(jax.random.fold_in(seeds[4], part), 71), part)
    site_mask = draw_site_mask(jax.random.fold_in(jax.random.fold_in(seeds[4], part), 71), part)
    couplings = draw_couplings(jax.random.fold_in(jax.random.fold_in(seeds[4], part), 71), part)
    target = draw_target(jax.random.fold_in(jax.random.fold_in(seeds[4], part), 71), part)
    return dict(probe_amplitudes=probe_amplitudes, site_mask=site_mask, couplings=couplings, target=target)


SCALE = 10.0


def kernel_table(count, points):
    order = jnp.arange(count).astype(jnp.float32)
    theta = jnp.pi * (jnp.arange(points).astype(jnp.float32) + 0.5) / points
    table = jnp.cos(order[:, None] * theta[None, :])
    total = count + 1.0
    jackson = ((total - order) * jnp.cos(jnp.pi * order / total) + jnp.sin(jnp.pi * order / total) / jnp.tan(jnp.pi / total)) / total
    doubled = jnp.where(jnp.arange(count) > 0, 2.0, 1.0).astype(jnp.float32)
    return table, doubled * jackson


def misfit_weights(moments, target):
    table, scaled = kernel_table(moments.shape[0], target.shape[0])
    spectrum = jnp.dot(scaled * moments, table, precision=lax.Precision.HIGHEST)
    misfit = spectrum - target
    return (2.0 / target.shape[0]) * scaled * jnp.dot(table, misfit, precision=lax.Precision.HIGHEST)


def bond_weights(present, couplings):
    return tuple(couplings[axis] * present * jnp.roll(present, -1, axis) for axis in range(3))


def operate(vector, bonds):
    total = bonds[0] * (vector - jnp.roll(vector, -1, 0)) + jnp.roll(bonds[0], 1, 0) * (vector - jnp.roll(vector, 1, 0))
    for axis in (1, 2):
        total = total + bonds[axis] * (vector - jnp.roll(vector, -1, axis)) + jnp.roll(bonds[axis], 1, axis) * (vector - jnp.roll(vector, 1, axis))
    return total / SCALE - vector


def chain(probe, bonds):
    states = [probe, operate(probe, bonds)]
    for step in range(1, STEPS):
        states.append(2.0 * operate(states[-1], bonds) - states[-2])
    return states


def bond_products(adjoint, state):
    return jnp.stack([(adjoint - jnp.roll(adjoint, -1, axis)) * (state - jnp.roll(state, -1, axis)) for axis in range(3)])


def reference(probe_amplitudes, site_mask, couplings, target):
    present = site_mask.astype(jnp.float32)
    bonds = bond_weights(present, couplings)
    count = probe_amplitudes.shape[0] * site_mask.shape[0] * site_mask.shape[1] * site_mask.shape[2]

    def probe_vector(amplitude):
        return amplitude * present

    def moment_step(carry, amplitude):
        probe = probe_vector(amplitude)
        states = chain(probe, bonds)
        return carry + jnp.stack([jnp.sum(probe * state) for state in states]), None

    totals, _ = lax.scan(moment_step, jnp.zeros((STEPS + 1,), jnp.float32), probe_amplitudes)
    moments = totals / count
    weights = misfit_weights(moments, target)

    def adjoint_step(carry, amplitude):
        probe = probe_vector(amplitude)
        states = chain(probe, bonds)
        later = weights[STEPS] * probe
        beyond = later
        products = jnp.zeros(couplings.shape, jnp.float32)
        for step in range(STEPS, 0, -1):
            image = operate(later, bonds)
            factor = 1.0 if step == 1 else 2.0
            products = products + factor * bond_products(later, states[step - 1])
            if step == STEPS:
                earlier = weights[step - 1] * probe + 2.0 * image
            elif step == 1:
                earlier = weights[0] * probe + image - beyond
            else:
                earlier = weights[step - 1] * probe + 2.0 * image - beyond
            beyond = later
            later = earlier
        costate = later
        for step in range(STEPS + 1):
            costate = costate + weights[step] * states[step]
        return carry + products, costate

    summed, costates = lax.scan(adjoint_step, jnp.zeros(couplings.shape, jnp.float32), probe_amplitudes)
    pairs = jnp.stack([present * jnp.roll(present, -1, axis) for axis in range(3)])
    return costates, pairs * summed / SCALE
```

```python
import functools

import jax
import jax.numpy as jnp
import numpy as np
from jax import lax
from jax.experimental import pallas as pl
from jax.experimental.pallas import tpu as pltpu
from jax.sharding import PartitionSpec as P

STEPS = 8
SCALE = 10.0
MESH = pl.DeviceIdType.MESH
ROWS = 16
LANES = 128


def tables(points):
    count = STEPS + 1
    order = np.arange(count)
    theta = np.pi * (np.arange(points) + 0.5) / points
    total = count + 1.0
    jackson = (
        (total - order) * np.cos(np.pi * order / total)
        + np.sin(np.pi * order / total) / np.tan(np.pi / total)
    ) / total
    table = np.zeros((ROWS, points), np.float32)
    table[:count] = np.cos(order[:, None] * theta[None, :])
    scaled = np.zeros((ROWS, LANES), np.float32)
    scaled[:count] = (np.where(order > 0, 2.0, 1.0) * jackson)[:, None]
    return table, scaled


def following(x, axis):
    return pltpu.roll(x, x.shape[axis] - 1, axis)


def preceding(x, axis):
    return pltpu.roll(x, 1, axis)


def flipped(index, bit):
    return index + bit - 2 * bit * lax.rem(lax.div(index, bit), 2)


def kernel(
    spaces, probes, total_sites,
    amp, mask, coup, target, table, scaled,
    costate, grad,
    v, du, q, g, bond, pair, low_product, high_mask, mom_a, mom_b, recv, direct,
    halo_send, halo_recv, edge_send, edge_recv,
    ma_send, ma_recv, mb_send, mb_recv, rs_send, rs_recv, d_send, d_recv,
):
    planes = mask.shape[0]
    last = planes - 1
    block = mask.shape[1] // probes
    s = lax.axis_index("space")
    p = lax.axis_index("probe")
    after, before = lax.rem(s + 1, spaces), lax.rem(s + spaces - 1, spaces)

    barrier = pltpu.get_barrier_semaphore()
    for off in range(1, spaces):
        pl.semaphore_signal(
            barrier, inc=1, device_id={"space": lax.rem(s + off, spaces)}, device_id_type=MESH
        )
    for off in range(1, probes):
        pl.semaphore_signal(
            barrier, inc=1, device_id={"probe": lax.rem(p + off, probes)}, device_id_type=MESH
        )

    started = []

    def send(src, dst, send_sem, recv_sem, where):
        copy = pltpu.make_async_remote_copy(
            src_ref=src, dst_ref=dst, send_sem=send_sem, recv_sem=recv_sem,
            device_id=where, device_id_type=MESH,
        )
        copy.start()
        started.append(copy)
        return copy

    for i in range(planes):
        v[0, i + 1] = amp[0, i] * mask[i]
    low_product[0] = (2.0 / SCALE) * (coup[0, last] * mask[last])
    pl.semaphore_wait(barrier, spaces + probes - 2)

    def send_low(k):
        return send(v.at[k, 1], v.at[k, planes + 1], halo_send.at[k, 0], halo_recv.at[k, 0], {"space": before})

    def send_high(k):
        return send(v.at[k, planes], v.at[k, 0], halo_send.at[k, 1], halo_recv.at[k, 1], {"space": after})

    edge_high = send(mask.at[0], high_mask.at[0], edge_send.at[0], edge_recv.at[0], {"space": before})
    edge_low = send(low_product.at[0], low_product.at[1], edge_send.at[1], edge_recv.at[1], {"space": after})
    from_high = send_low(0)
    from_low = send_high(0)

    for i in range(planes):
        m = mask[i]
        tenth = m * (1.0 / SCALE)
        if i < last:
            pair[0, i] = tenth * mask[i + 1]
            bond[0, i + 1] = 2.0 * coup[0, i] * pair[0, i]
        pair[1, i] = tenth * following(m, 0)
        pair[2, i] = tenth * following(m, 1)
        bond[1, i + 1] = 2.0 * coup[1, i] * pair[1, i]
        bond[2, i + 1] = 2.0 * coup[2, i] * pair[2, i]

    def moment(n, i, j):
        acc = v[i, 1] * v[j, 1]
        for plane in range(2, planes + 1):
            acc = acc + v[i, plane] * v[j, plane]
        row = jnp.sum(acc, axis=0, keepdims=True)
        part = row[:, :LANES]
        for start in range(LANES, row.shape[1], LANES):
            part = part + row[:, start:start + LANES]
        mom_a[p, pl.ds(n, 1), :] = part

    def product(n, d, i):
        acc = None
        for a in range(n // 2 + 1):
            term = du[d, a, i] * du[d, n - a, i]
            if a != n - a:
                term = 2.0 * term
            acc = term if acc is None else acc + term
        return acc

    def place(d, i):
        if d == 0:
            return 2 * planes + i
        return (d - 1) * planes + i

    sums = [None]

    def total_products(d, i, upto):
        acc = sums[0][1] * q[0, place(d, i)]
        for n in range(1, upto + 1):
            acc = acc + sums[0][n + 1] * q[n, place(d, i)]
        return acc

    mom_a[p, pl.ds(8, 8), :] = jnp.zeros((8, LANES), jnp.float32)
    a_copies, b_copies = [], []
    early = 3 * planes - 1
    rs_copies = {}
    weights = None

    def rows_of(index):
        return pl.ds(pl.multiple_of(index * block, block), block)

    def rs_start(level):
        bit = 1 << level
        other = flipped(p, bit)
        copies = []
        for j in range(probes // (2 * bit)):
            index = lax.rem(other, 2 * bit) + j * 2 * bit
            copies.append(send(
                g.at[pl.ds(0, early), rows_of(index)],
                recv.at[level, j],
                rs_send.at[level, j], rs_recv.at[level, j], {"probe": other},
            ))
        rs_copies[level] = copies

    def rs_finish(level):
        bit = 1 << level
        for j, copy in enumerate(rs_copies[level]):
            copy.wait_recv()
            index = lax.rem(p, 2 * bit) + j * 2 * bit
            g[pl.ds(0, early), rows_of(index)] = g[pl.ds(0, early), rows_of(index)] + recv[level, j]

    levels = probes.bit_length() - 1

    for k in range(STEPS):
        factor = 1.0 if k == 0 else 2.0
        across = [v[k, i + 1] - v[k, i + 2] for i in range(last)]
        for i in range(last):
            du[0, k, i] = factor * across[i]
        for i in range(planes):
            here = v[k, i + 1]
            d1 = here - following(here, 0)
            d2 = here - following(here, 1)
            du[1, k, i] = factor * d1
            du[2, k, i] = factor * d2
            f1 = bond[1, i + 1] * d1
            f2 = bond[2, i + 1] * d2
            inside = (f1 - preceding(f1, 0)) + (f2 - preceding(f2, 1))
            if i < last:
                inside = inside + bond[0, i + 1] * across[i]
            if i > 0:
                inside = inside - bond[0, i] * across[i - 1]
            if k == 0:
                v[1, i + 1] = 0.5 * inside - here
            else:
                v[k + 1, i + 1] = inside - 2.0 * here - v[k - 1, i + 1]

        if k <= 4:
            if k == 0:
                moment(0, 0, 0)
            else:
                moment(2 * k - 1, k - 1, k)
                moment(2 * k, k, k)
        if k == 4:
            for off in range(1, probes):
                a_copies.append(send(
                    mom_a.at[p], mom_a.at[p], ma_send.at[off], ma_recv.at[off],
                    {"probe": lax.rem(p + off, probes)},
                ))
        if k == 5:
            for copy in a_copies:
                copy.wait_recv()
            acc = mom_a[0]
            for index in range(1, probes):
                acc = acc + mom_a[index]
            mom_b[s] = acc
            for off in range(1, spaces):
                b_copies.append(send(
                    mom_b.at[s], mom_b.at[s], mb_send.at[off], mb_recv.at[off],
                    {"space": lax.rem(s + off, spaces)},
                ))
        if k == 6:
            for copy in b_copies:
                copy.wait_recv()
            acc = mom_b[0]
            for index in range(1, spaces):
                acc = acc + mom_b[index]
            raw = jnp.sum(acc, axis=1, keepdims=True) / total_sites
            base0, base1 = raw[0:1], raw[1:2]
            moments = [base0, base1]
            for n in range(2, STEPS + 1):
                moments.append(2.0 * raw[n:n + 1] - (base0 if n % 2 == 0 else base1))
            points = target.shape[1]
            spectrum = jnp.zeros((1, points), jnp.float32)
            for n in range(STEPS + 1):
                spectrum = spectrum + scaled[n:n + 1, 0:1] * moments[n] * table[n:n + 1, :]
            misfit = spectrum - target[...]
            weights = []
            for n in range(STEPS + 1):
                dot = jnp.sum(table[n:n + 1, :] * misfit, axis=1, keepdims=True)
                weights.append((2.0 / points) * scaled[n:n + 1, 0:1] * dot)
            partial = [None] * (STEPS + 1)
            for n in range(STEPS, 0, -1):
                partial[n] = weights[n] if n + 2 > STEPS else weights[n] + partial[n + 2]
            sums[0] = partial

        for d, i in [(d, i) for d in (1, 2, 0) for i in range(planes)]:
            if d == 0 and i == last:
                continue
            if k < STEPS - 1:
                q[k, place(d, i)] = product(k, d, i)
            else:
                whole = total_products(d, i, k - 1) + sums[0][k + 1] * product(k, d, i)
                g[place(d, i)] = pair[d, i] * whole
        if k == STEPS - 1:
            rs_start(0)
            for i in range(planes):
                acc = weights[0] * v[0, i + 1]
                for n in range(1, STEPS):
                    acc = acc + weights[n] * v[n, i + 1]
                costate[0, i] = 2.0 * acc
            for level in range(levels):
                rs_finish(level)
                if level + 1 < levels:
                    rs_start(level + 1)

        if k == 0:
            edge_high.wait_recv()
            pair[0, last] = mask[last] * (1.0 / SCALE) * high_mask[0]
            bond[0, planes] = 2.0 * coup[0, last] * pair[0, last]
            edge_low.wait_recv()
            bond[0, 0] = low_product[1] * mask[0]
        share = 0.5 if k == 0 else 1.0
        from_high.wait_recv()
        top = v[k, planes] - v[k, planes + 1]
        v[k + 1, planes] = v[k + 1, planes] + share * bond[0, planes] * top
        if k + 1 < STEPS:
            next_low = send_high(k + 1)
        du[0, k, last] = factor * top
        from_low.wait_recv()
        bottom = v[k, 0] - v[k, 1]
        v[k + 1, 1] = v[k + 1, 1] - share * bond[0, 0] * bottom
        if k + 1 < STEPS:
            next_high = send_low(k + 1)
            from_high, from_low = next_high, next_low
            q[k, place(0, last)] = product(k, 0, last)

    k = STEPS - 1
    whole = total_products(0, last, k - 1) + sums[0][k + 1] * product(k, 0, last)
    g[early] = pair[0, last] * whole
    d_copies = []
    for off in range(1, probes):
        other = lax.rem(p + off, probes)
        d_copies.append(send(
            g.at[early, rows_of(other)], direct.at[off - 1], d_send.at[off], d_recv.at[off],
            {"probe": other},
        ))
    for i in range(planes):
        costate[0, i] = costate[0, i] + 2.0 * weights[STEPS] * v[STEPS, i + 1]
    for d, i in [(d, i) for d in (1, 2, 0) for i in range(planes)]:
        if d == 0 and i == last:
            continue
        grad[d, i] = g[place(d, i), rows_of(p)]
    acc = g[early, rows_of(p)]
    for off in range(1, probes):
        d_copies[off - 1].wait_recv()
        acc = acc + direct[off - 1]
    grad[0, last] = acc
    for copy in started:
        copy.wait_send()


def on_device(probe_amplitudes, site_mask, couplings, target):
    spaces, probes = lax.axis_size("space"), lax.axis_size("probe")
    planes, rows, lanes = site_mask.shape
    table, scaled = tables(target.shape[0])
    block = rows // probes
    levels = probes.bit_length() - 1
    f32 = jnp.float32
    total_sites = float(probes * spaces * planes * rows * lanes)
    vmem = pl.BlockSpec(memory_space=pltpu.VMEM)
    dma = pltpu.SemaphoreType.DMA
    return pl.pallas_call(
        functools.partial(kernel, spaces, probes, total_sites),
        out_shape=(
            jax.ShapeDtypeStruct((1, planes, rows, lanes), f32),
            jax.ShapeDtypeStruct((3, planes, block, lanes), f32),
        ),
        in_specs=[vmem] * 6,
        out_specs=(vmem, vmem),
        scratch_shapes=[
            pltpu.VMEM((STEPS + 1, planes + 2, rows, lanes), f32),
            pltpu.VMEM((3, STEPS, planes, rows, lanes), f32),
            pltpu.VMEM((STEPS, 3 * planes, rows, lanes), f32),
            pltpu.VMEM((3 * planes, rows, lanes), f32),
            pltpu.VMEM((3, planes + 1, rows, lanes), f32),
            pltpu.VMEM((3, planes, rows, lanes), f32),
            pltpu.VMEM((2, rows, lanes), f32),
            pltpu.VMEM((1, rows, lanes), f32),
            pltpu.VMEM((probes, ROWS, LANES), f32),
            pltpu.VMEM((spaces, ROWS, LANES), f32),
            pltpu.VMEM((levels, probes // 2, 3 * planes - 1, block, lanes), f32),
            pltpu.VMEM((probes - 1, block, lanes), f32),
            dma((STEPS, 2)), dma((STEPS, 2)), dma((2,)), dma((2,)),
            dma((probes,)), dma((probes,)), dma((spaces,)), dma((spaces,)),
            dma((levels, probes // 2)), dma((levels, probes // 2)),
            dma((probes,)), dma((probes,)),
        ],
        compiler_params=pltpu.CompilerParams(
            collective_id=0, has_side_effects=True, vmem_limit_bytes=48 * 1024 * 1024
        ),
    )(probe_amplitudes, site_mask, couplings, target[None], table, scaled)


def solution(mesh):
    return jax.shard_map(
        on_device,
        mesh=mesh,
        in_specs=(
            P(("groups", "probe"), "space", None, None),
            P(("groups", "space"), None, None),
            P(None, ("groups", "space"), None, None),
            P("groups"),
        ),
        out_specs=(
            P(("groups", "probe"), "space", None, None),
            P(None, ("groups", "space"), "probe", None),
        ),
        check_vma=False,
    )
```

```python
import functools

import jax
import jax.numpy as jnp
import numpy as np
from jax import lax
from jax.experimental import pallas as pl
from jax.experimental.pallas import tpu as pltpu
from jax.sharding import PartitionSpec as P

STEPS = 8
SCALE = 10.0
MESH = pl.DeviceIdType.MESH
ROWS = 16
LANES = 128


def tables(points):
    count = STEPS + 1
    order = np.arange(count)
    theta = np.pi * (np.arange(points) + 0.5) / points
    total = count + 1.0
    jackson = (
        (total - order) * np.cos(np.pi * order / total)
        + np.sin(np.pi * order / total) / np.tan(np.pi / total)
    ) / total
    table = np.zeros((ROWS, points), np.float32)
    table[:count] = np.cos(order[:, None] * theta[None, :])
    scaled = np.zeros((ROWS, LANES), np.float32)
    scaled[:count] = (np.where(order > 0, 2.0, 1.0) * jackson)[:, None]
    return table, scaled


def following(x, axis):
    return pltpu.roll(x, x.shape[axis] - 1, axis)


def preceding(x, axis):
    return pltpu.roll(x, 1, axis)


def flipped(index, bit):
    return index + bit - 2 * bit * lax.rem(lax.div(index, bit), 2)


def kernel(
    spaces, probes, total_sites,
    amp_in, mask_in, coup_in, target_in, table_in, scaled_in,
    costate, grad,
    amp, mask, coup, target, table, scaled,
    v, du, q, g, bond, pair, give, got, mom_a, mom_b, recv, direct,
    load_sem, edge_send, edge_recv, mid_send, mid_recv,
    give_send, give_recv, pass_send, pass_recv,
    ma_send, ma_recv, mb_send, mb_recv, rs_send, rs_recv, d_send, d_recv,
):
    planes, rows, _ = mask.shape
    first, last, high = 2, planes + 1, planes + 2
    middle = 3
    block = rows // probes
    half = rows // 2
    s = lax.axis_index("space")
    p = lax.axis_index("probe")
    after, before = lax.rem(s + 1, spaces), lax.rem(s + spaces - 1, spaces)
    twin = flipped(p, 1)

    loads = []
    for n, (src, dst) in enumerate([
        (mask_in, mask), (amp_in, amp), (coup_in, coup),
        (target_in, target), (table_in, table), (scaled_in, scaled),
    ]):
        loads.append(pltpu.make_async_copy(src, dst, load_sem.at[n]))
        loads[-1].start()
    barrier = pltpu.get_barrier_semaphore()
    for off in range(1, spaces):
        pl.semaphore_signal(
            barrier, inc=1, device_id={"space": lax.rem(s + off, spaces)}, device_id_type=MESH
        )
    for off in range(1, probes):
        pl.semaphore_signal(
            barrier, inc=1, device_id={"probe": lax.rem(p + off, probes)}, device_id_type=MESH
        )

    started = []

    def send(src, dst, send_sem, recv_sem, where):
        copy = pltpu.make_async_remote_copy(
            src_ref=src, dst_ref=dst, send_sem=send_sem, recv_sem=recv_sem,
            device_id=where, device_id_type=MESH,
        )
        copy.start()
        started.append(copy)
        return copy

    low_mid, high_mid = {}, {}

    def send_middle(k):
        low_mid[k] = send(
            v.at[k, middle], v.at[k, 0], mid_send.at[k, 0], mid_recv.at[k, 0], {"space": after}
        )
        high_mid[k] = send(
            v.at[k, middle], v.at[k, high + 1], mid_send.at[k, 1], mid_recv.at[k, 1], {"space": before}
        )

    own_half = pl.ds(pl.multiple_of(lax.rem(p, 2) * half, half), half)

    def send_bonds(group, start, size):
        out = []
        for side, where in ((0, after), (1, before)):
            out.append(send(
                give.at[side, pl.ds(start, size), own_half],
                got.at[side, pl.ds(start, size), own_half],
                give_send.at[group, side], give_recv.at[group, side], {"space": where},
            ))
        return out

    def pass_bonds(group, start, size, copies):
        out = []
        for side in (0, 1):
            copies[side].wait_recv()
            out.append(send(
                got.at[side, pl.ds(start, size), own_half],
                got.at[side, pl.ds(start, size), own_half],
                pass_send.at[group, side], pass_recv.at[group, side], {"probe": twin},
            ))
        return out

    for n in (0, 1):
        loads[n].wait()
    for i in range(planes):
        v[0, first + i] = amp[0, i] * mask[i]
    pl.semaphore_wait(barrier, spaces + probes - 2)
    edge_low = send(v.at[0, last], v.at[0, 1], edge_send.at[0], edge_recv.at[0], {"space": after})
    edge_high = send(v.at[0, first], v.at[0, high], edge_send.at[1], edge_recv.at[1], {"space": before})
    loads[2].wait()
    give[0, 0] = (2.0 / SCALE) * (coup[0, planes - 1] * mask[planes - 1])
    give[1, 0] = mask[0]
    near = send_bonds(0, 0, 1)
    send_middle(0)

    for i in range(planes):
        m = mask[i]
        tenth = m * (1.0 / SCALE)
        if i < planes - 1:
            pair[0, i] = tenth * mask[i + 1]
            bond[0, first + i] = 2.0 * coup[0, i] * pair[0, i]
        pair[1, i] = tenth * following(m, 0)
        pair[2, i] = tenth * following(m, 1)
        for d in (1, 2):
            bond[d, first + i] = 2.0 * coup[d, i] * pair[d, i]
    give[0, 1] = bond[0, last - 1]
    give[1, 1] = bond[0, first]
    for d in (1, 2):
        give[0, d + 1] = bond[d, last]
        give[1, d + 1] = bond[d, first]
    far = send_bonds(1, 1, 3)

    def strength(d, j):
        if d == 0 and j == 0:
            return got[0, 1]
        if d == 0 and j == high:
            return got[1, 1]
        if d > 0 and j == 1:
            return got[0, d + 1]
        if d > 0 and j == high:
            return got[1, d + 1]
        return bond[d, j]

    def factor(k):
        return 1.0 if k == 0 else 2.0

    def step(k, j):
        here = v[k, j]
        d0 = here - v[k, j + 1]
        d1 = here - following(here, 0)
        d2 = here - following(here, 1)
        f1 = strength(1, j) * d1
        f2 = strength(2, j) * d2
        inside = (f1 - preceding(f1, 0)) + (f2 - preceding(f2, 1))
        inside = inside + strength(0, j) * d0
        inside = inside + strength(0, j - 1) * (here - v[k, j - 1])
        if k == 0:
            v[1, j] = 0.5 * inside - here
        else:
            v[k + 1, j] = inside - 2.0 * here - v[k - 1, j]
        if first <= j <= last and k < STEPS - 1:
            du[0, k, j - first] = factor(k) * d0
            du[1, k, j - first] = factor(k) * d1
            du[2, k, j - first] = factor(k) * d2

    def moment(n, i, j):
        acc = v[i, first] * v[j, first]
        for plane in range(first + 1, last + 1):
            acc = acc + v[i, plane] * v[j, plane]
        row = jnp.sum(acc, axis=0, keepdims=True)
        part = row[:, :LANES]
        for start in range(LANES, row.shape[1], LANES):
            part = part + row[:, start:start + LANES]
        mom_a[p, pl.ds(n, 1), :] = part

    def product(n, d, i):
        acc = None
        for a in range(n // 2 + 1):
            term = du[d, a, i] * du[d, n - a, i]
            if a != n - a:
                term = 2.0 * term
            acc = term if acc is None else acc + term
        return acc

    def place(d, i):
        if d == 0:
            return 2 * planes + i
        return (d - 1) * planes + i

    every = [(d, i) for d in (1, 2, 0) for i in range(planes)]
    early = 3 * planes - 1

    def products(n):
        for d, i in every:
            q[n, place(d, i)] = product(n, d, i)

    def gradient(d, i, sums):
        acc = sums[STEPS] * product(STEPS - 1, d, i)
        for n in range(STEPS - 1):
            acc = acc + sums[n + 1] * q[n, place(d, i)]
        g[place(d, i)] = pair[d, i] * acc

    def rows_of(index):
        return pl.ds(pl.multiple_of(index * block, block), block)

    levels = probes.bit_length() - 1
    rs_copies = {}

    def rs_start(level):
        bit = 1 << level
        other = flipped(p, bit)
        rs_copies[level] = []
        for j in range(probes // (2 * bit)):
            index = lax.rem(other, 2 * bit) + j * 2 * bit
            rs_copies[level].append(send(
                g.at[pl.ds(0, early), rows_of(index)], recv.at[level, j],
                rs_send.at[level, j], rs_recv.at[level, j], {"probe": other},
            ))

    def rs_finish(level):
        bit = 1 << level
        for j, copy in enumerate(rs_copies[level]):
            copy.wait_recv()
            index = lax.rem(p, 2 * bit) + j * 2 * bit
            g[pl.ds(0, early), rows_of(index)] = g[pl.ds(0, early), rows_of(index)] + recv[level, j]

    step(0, middle)
    send_middle(1)
    near = pass_bonds(0, 0, 1, near)
    mom_a[p, pl.ds(8, 8), :] = jnp.zeros((8, LANES), jnp.float32)
    moment(0, 0, 0)
    for copy in near:
        copy.wait_recv()
    bond[0, 1] = got[0, 0] * mask[0]
    pair[0, planes - 1] = mask[planes - 1] * (1.0 / SCALE) * got[1, 0]
    bond[0, last] = 2.0 * coup[0, planes - 1] * pair[0, planes - 1]
    edge_low.wait_recv()
    step(0, first)
    edge_high.wait_recv()
    step(0, last)
    step(1, middle)
    send_middle(2)
    far = pass_bonds(1, 1, 3, far)
    moment(1, 0, 1)
    moment(2, 1, 1)
    products(0)
    for copy in far:
        copy.wait_recv()

    a_copies, b_copies = [], []
    weights, sums = None, None
    for t in range(STEPS - 1):
        low_mid[t].wait_recv()
        step(t, 1)
        step(t + 1, first)
        high_mid[t].wait_recv()
        step(t, high)
        step(t + 1, last)
        if t + 2 < STEPS:
            step(t + 2, middle)
        if t + 3 < STEPS - 1:
            send_middle(t + 3)

        if t < 3:
            moment(2 * t + 3, t + 1, t + 2)
            moment(2 * t + 4, t + 2, t + 2)
        if t == 2:
            for off in range(1, probes):
                a_copies.append(send(
                    mom_a.at[p], mom_a.at[p], ma_send.at[off], ma_recv.at[off],
                    {"probe": lax.rem(p + off, probes)},
                ))
        if t == 3:
            for copy in a_copies:
                copy.wait_recv()
            acc = mom_a[0]
            for index in range(1, probes):
                acc = acc + mom_a[index]
            mom_b[s] = acc
            for off in range(1, spaces):
                b_copies.append(send(
                    mom_b.at[s], mom_b.at[s], mb_send.at[off], mb_recv.at[off],
                    {"space": lax.rem(s + off, spaces)},
                ))
        if t < STEPS - 2:
            products(t + 1)
        if t == STEPS - 3:
            for n in (3, 4, 5):
                loads[n].wait()
            for copy in b_copies:
                copy.wait_recv()
            acc = mom_b[0]
            for index in range(1, spaces):
                acc = acc + mom_b[index]
            raw = jnp.sum(acc, axis=1, keepdims=True) / total_sites
            base = (raw[0:1], raw[1:2])
            moments = list(base)
            for n in range(2, STEPS + 1):
                moments.append(2.0 * raw[n:n + 1] - base[n % 2])
            points = target.shape[1]
            spectrum = jnp.zeros((1, points), jnp.float32)
            for n in range(STEPS + 1):
                spectrum = spectrum + scaled[n:n + 1, 0:1] * moments[n] * table[n:n + 1, :]
            misfit = spectrum - target[...]
            weights = []
            for n in range(STEPS + 1):
                dot = jnp.sum(table[n:n + 1, :] * misfit, axis=1, keepdims=True)
                weights.append((2.0 / points) * scaled[n:n + 1, 0:1] * dot)
            sums = [None] * (STEPS + 1)
            for n in range(STEPS, 0, -1):
                sums[n] = weights[n] if n + 2 > STEPS else weights[n] + sums[n + 2]
            k = STEPS - 1
            for i in range(planes):
                here = v[k, first + i]
                du[1, k, i] = 2.0 * (here - following(here, 0))
                du[2, k, i] = 2.0 * (here - following(here, 1))
                if i < planes - 1:
                    du[0, k, i] = 2.0 * (here - v[k, first + i + 1])
            for d, i in every[:-1]:
                gradient(d, i, sums)
            rs_start(0)
            for i in range(planes):
                acc = weights[0] * v[0, first + i]
                for n in range(1, STEPS):
                    acc = acc + weights[n] * v[n, first + i]
                costate[0, i] = 2.0 * acc
            rs_finish(0)
            if levels > 1:
                rs_start(1)

    k = STEPS - 1
    du[0, k, planes - 1] = 2.0 * (v[k, last] - v[k, high])
    gradient(0, planes - 1, sums)
    d_copies = []
    for off in range(1, probes):
        other = lax.rem(p + off, probes)
        d_copies.append(send(
            g.at[early, rows_of(other)], direct.at[off - 1], d_send.at[off], d_recv.at[off],
            {"probe": other},
        ))
    for i in range(planes):
        costate[0, i] = costate[0, i] + 2.0 * weights[STEPS] * v[STEPS, first + i]
    for level in range(1, levels):
        rs_finish(level)
        if level + 1 < levels:
            rs_start(level + 1)
    for d, i in every[:-1]:
        grad[d, i] = g[place(d, i), rows_of(p)]
    acc = g[early, rows_of(p)]
    for off in range(1, probes):
        d_copies[off - 1].wait_recv()
        acc = acc + direct[off - 1]
    grad[0, planes - 1] = acc
    for copy in started:
        copy.wait_send()


def on_device(probe_amplitudes, site_mask, couplings, target):
    spaces, probes = lax.axis_size("space"), lax.axis_size("probe")
    planes, rows, lanes = site_mask.shape
    table, scaled = tables(target.shape[0])
    block = rows // probes
    levels = probes.bit_length() - 1
    f32 = jnp.float32
    total_sites = float(probes * spaces * planes * rows * lanes)
    vmem = pl.BlockSpec(memory_space=pltpu.VMEM)
    dma = pltpu.SemaphoreType.DMA
    return pl.pallas_call(
        functools.partial(kernel, spaces, probes, total_sites),
        out_shape=(
            jax.ShapeDtypeStruct((1, planes, rows, lanes), f32),
            jax.ShapeDtypeStruct((3, planes, block, lanes), f32),
        ),
        in_specs=[pl.BlockSpec(memory_space=pl.ANY)] * 6,
        out_specs=(vmem, vmem),
        scratch_shapes=[
            pltpu.VMEM(probe_amplitudes.shape, f32),
            pltpu.VMEM(site_mask.shape, f32),
            pltpu.VMEM(couplings.shape, f32),
            pltpu.VMEM((1, target.shape[0]), f32),
            pltpu.VMEM(table.shape, f32),
            pltpu.VMEM(scaled.shape, f32),
            pltpu.VMEM((STEPS + 1, planes + 4, rows, lanes), f32),
            pltpu.VMEM((3, STEPS, planes, rows, lanes), f32),
            pltpu.VMEM((STEPS, 3 * planes, rows, lanes), f32),
            pltpu.VMEM((3 * planes, rows, lanes), f32),
            pltpu.VMEM((3, planes + 3, rows, lanes), f32),
            pltpu.VMEM((3, planes, rows, lanes), f32),
            pltpu.VMEM((2, 4, rows, lanes), f32),
            pltpu.VMEM((2, 4, rows, lanes), f32),
            pltpu.VMEM((probes, ROWS, LANES), f32),
            pltpu.VMEM((spaces, ROWS, LANES), f32),
            pltpu.VMEM((levels, probes // 2, 3 * planes - 1, block, lanes), f32),
            pltpu.VMEM((probes - 1, block, lanes), f32),
            dma((6,)), dma((2,)), dma((2,)), dma((STEPS, 2)), dma((STEPS, 2)),
            dma((2, 2)), dma((2, 2)), dma((2, 2)), dma((2, 2)),
            dma((probes,)), dma((probes,)), dma((spaces,)), dma((spaces,)),
            dma((levels, probes // 2)), dma((levels, probes // 2)),
            dma((probes,)), dma((probes,)),
        ],
        compiler_params=pltpu.CompilerParams(
            collective_id=0, has_side_effects=True, vmem_limit_bytes=48 * 1024 * 1024
        ),
    )(probe_amplitudes, site_mask, couplings, target[None], table, scaled)


def solution(mesh):
    return jax.shard_map(
        on_device,
        mesh=mesh,
        in_specs=(
            P(("groups", "probe"), "space", None, None),
            P(("groups", "space"), None, None),
            P(None, ("groups", "space"), None, None),
            P("groups"),
        ),
        out_specs=(
            P(("groups", "probe"), "space", None, None),
            P(None, ("groups", "space"), "probe", None),
        ),
        check_vma=False,
    )
```

```python
import functools

import jax
import jax.numpy as jnp
import numpy as np
from jax import lax
from jax.experimental import pallas as pl
from jax.experimental.pallas import tpu as pltpu
from jax.sharding import PartitionSpec as P

STEPS = 8
SCALE = 10.0
MESH = pl.DeviceIdType.MESH
ROWS = 16
LANES = 128


def tables(points):
    count = STEPS + 1
    order = np.arange(count)
    theta = np.pi * (np.arange(points) + 0.5) / points
    total = count + 1.0
    jackson = (
        (total - order) * np.cos(np.pi * order / total)
        + np.sin(np.pi * order / total) / np.tan(np.pi / total)
    ) / total
    table = np.zeros((ROWS, points), np.float32)
    table[:count] = np.cos(order[:, None] * theta[None, :])
    scaled = np.zeros((ROWS, LANES), np.float32)
    scaled[:count] = (np.where(order > 0, 2.0, 1.0) * jackson)[:, None]
    return table, scaled


def following(x, axis):
    return pltpu.roll(x, x.shape[axis] - 1, axis)


def preceding(x, axis):
    return pltpu.roll(x, 1, axis)


def flipped(index, bit):
    return index + bit - 2 * bit * lax.rem(lax.div(index, bit), 2)


def kernel(
    spaces, probes, total_sites,
    amp_in, mask_in, coup_in, target_in, table_in, scaled_in,
    costate_out, grad_out,
    costate, grad, amp, mask, coup, target, table, scaled,
    v, du, q, g, bond, pair, give, got, mom_a, mom_b, recv, direct,
    load_sem, edge_send, edge_recv, mid_send, mid_recv,
    give_send, give_recv, pass_send, pass_recv,
    ma_send, ma_recv, mb_send, mb_recv, rs_send, rs_recv, d_send, d_recv,
):
    planes, rows, _ = mask.shape
    first, last, high = 2, planes + 1, planes + 2
    middle = 3
    block = rows // probes
    half = rows // 2
    s = lax.axis_index("space")
    p = lax.axis_index("probe")
    after, before = lax.rem(s + 1, spaces), lax.rem(s + spaces - 1, spaces)
    twin = flipped(p, 1)

    loads = []
    for n, (src, dst) in enumerate([
        (mask_in, mask), (amp_in, amp), (coup_in, coup),
        (target_in, target), (table_in, table), (scaled_in, scaled),
    ]):
        loads.append(pltpu.make_async_copy(src, dst, load_sem.at[n]))
        loads[-1].start()
    barrier = pltpu.get_barrier_semaphore()
    for off in range(1, spaces):
        pl.semaphore_signal(
            barrier, inc=1, device_id={"space": lax.rem(s + off, spaces)}, device_id_type=MESH
        )
    for off in range(1, probes):
        pl.semaphore_signal(
            barrier, inc=1, device_id={"probe": lax.rem(p + off, probes)}, device_id_type=MESH
        )

    started = []

    def send(src, dst, send_sem, recv_sem, where):
        copy = pltpu.make_async_remote_copy(
            src_ref=src, dst_ref=dst, send_sem=send_sem, recv_sem=recv_sem,
            device_id=where, device_id_type=MESH,
        )
        copy.start()
        started.append(copy)
        return copy

    low_mid, high_mid = {}, {}

    def send_middle(k):
        low_mid[k] = send(
            v.at[k, middle], v.at[k, 0], mid_send.at[k, 0], mid_recv.at[k, 0], {"space": after}
        )
        high_mid[k] = send(
            v.at[k, middle], v.at[k, high + 1], mid_send.at[k, 1], mid_recv.at[k, 1], {"space": before}
        )

    own_half = pl.ds(pl.multiple_of(lax.rem(p, 2) * half, half), half)

    def send_bonds(group, start, size):
        out = []
        for side, where in ((0, after), (1, before)):
            out.append(send(
                give.at[side, pl.ds(start, size), own_half],
                got.at[side, pl.ds(start, size), own_half],
                give_send.at[group, side], give_recv.at[group, side], {"space": where},
            ))
        return out

    def pass_bonds(group, start, size, copies):
        out = []
        for side in (0, 1):
            copies[side].wait_recv()
            out.append(send(
                got.at[side, pl.ds(start, size), own_half],
                got.at[side, pl.ds(start, size), own_half],
                pass_send.at[group, side], pass_recv.at[group, side], {"probe": twin},
            ))
        return out

    for n in (0, 1):
        loads[n].wait()
    for i in range(planes):
        v[0, first + i] = amp[0, i] * mask[i]
    pl.semaphore_wait(barrier, spaces + probes - 2)
    edge_low = send(v.at[0, last], v.at[0, 1], edge_send.at[0], edge_recv.at[0], {"space": after})
    edge_high = send(v.at[0, first], v.at[0, high], edge_send.at[1], edge_recv.at[1], {"space": before})
    loads[2].wait()
    give[0, 0] = (2.0 / SCALE) * (coup[0, planes - 1] * mask[planes - 1])
    give[1, 0] = mask[0]
    near = send_bonds(0, 0, 1)
    send_middle(0)

    for i in range(planes):
        m = mask[i]
        tenth = m * (1.0 / SCALE)
        if i < planes - 1:
            pair[0, i] = tenth * mask[i + 1]
            bond[0, first + i] = 2.0 * coup[0, i] * pair[0, i]
        pair[1, i] = tenth * following(m, 0)
        pair[2, i] = tenth * following(m, 1)
        for d in (1, 2):
            bond[d, first + i] = 2.0 * coup[d, i] * pair[d, i]
    give[0, 1] = bond[0, last - 1]
    give[1, 1] = bond[0, first]
    for d in (1, 2):
        give[0, d + 1] = bond[d, last]
        give[1, d + 1] = bond[d, first]
    far = send_bonds(1, 1, 3)

    def strength(d, j):
        if d == 0 and j == 0:
            return got[0, 1]
        if d == 0 and j == high:
            return got[1, 1]
        if d > 0 and j == 1:
            return got[0, d + 1]
        if d > 0 and j == high:
            return got[1, d + 1]
        return bond[d, j]

    def factor(k):
        return 1.0 if k == 0 else 2.0

    def step(k, j):
        here = v[k, j]
        d0 = here - v[k, j + 1]
        d1 = here - following(here, 0)
        d2 = here - following(here, 1)
        f1 = strength(1, j) * d1
        f2 = strength(2, j) * d2
        inside = (f1 - preceding(f1, 0)) + (f2 - preceding(f2, 1))
        inside = inside + strength(0, j) * d0
        inside = inside + strength(0, j - 1) * (here - v[k, j - 1])
        if k == 0:
            v[1, j] = 0.5 * inside - here
        else:
            v[k + 1, j] = inside - 2.0 * here - v[k - 1, j]
        if first <= j <= last and k < STEPS - 1:
            du[0, k, j - first] = factor(k) * d0
            du[1, k, j - first] = factor(k) * d1
            du[2, k, j - first] = factor(k) * d2

    def moment(n, i, j):
        acc = v[i, first] * v[j, first]
        for plane in range(first + 1, last + 1):
            acc = acc + v[i, plane] * v[j, plane]
        row = jnp.sum(acc, axis=0, keepdims=True)
        part = row[:, :LANES]
        for start in range(LANES, row.shape[1], LANES):
            part = part + row[:, start:start + LANES]
        mom_a[p, pl.ds(n, 1), :] = part

    def product(n, d, i):
        acc = None
        for a in range(n // 2 + 1):
            term = du[d, a, i] * du[d, n - a, i]
            if a != n - a:
                term = 2.0 * term
            acc = term if acc is None else acc + term
        return acc

    def place(d, i):
        if d == 0:
            return 2 * planes + i
        return (d - 1) * planes + i

    every = [(d, i) for d in (1, 2, 0) for i in range(planes)]
    early = 3 * planes - 1

    def products(n):
        for d, i in every:
            q[n, place(d, i)] = product(n, d, i)

    def gradient(d, i, sums):
        acc = sums[STEPS] * product(STEPS - 1, d, i)
        for n in range(STEPS - 1):
            acc = acc + sums[n + 1] * q[n, place(d, i)]
        g[place(d, i)] = pair[d, i] * acc

    def rows_of(index):
        return pl.ds(pl.multiple_of(index * block, block), block)

    levels = probes.bit_length() - 1
    rs_copies = {}

    def rs_start(level):
        bit = 1 << level
        other = flipped(p, bit)
        rs_copies[level] = []
        for j in range(probes // (2 * bit)):
            index = lax.rem(other, 2 * bit) + j * 2 * bit
            rs_copies[level].append(send(
                g.at[pl.ds(0, early), rows_of(index)], recv.at[level, j],
                rs_send.at[level, j], rs_recv.at[level, j], {"probe": other},
            ))

    def rs_finish(level):
        bit = 1 << level
        for j, copy in enumerate(rs_copies[level]):
            copy.wait_recv()
            index = lax.rem(p, 2 * bit) + j * 2 * bit
            g[pl.ds(0, early), rows_of(index)] = g[pl.ds(0, early), rows_of(index)] + recv[level, j]

    step(0, middle)
    send_middle(1)
    near = pass_bonds(0, 0, 1, near)
    mom_a[p, pl.ds(8, 8), :] = jnp.zeros((8, LANES), jnp.float32)
    moment(0, 0, 0)
    for copy in near:
        copy.wait_recv()
    bond[0, 1] = got[0, 0] * mask[0]
    pair[0, planes - 1] = mask[planes - 1] * (1.0 / SCALE) * got[1, 0]
    bond[0, last] = 2.0 * coup[0, planes - 1] * pair[0, planes - 1]
    edge_low.wait_recv()
    step(0, first)
    edge_high.wait_recv()
    step(0, last)
    step(1, middle)
    send_middle(2)
    far = pass_bonds(1, 1, 3, far)
    moment(1, 0, 1)
    moment(2, 1, 1)
    products(0)
    for copy in far:
        copy.wait_recv()

    a_copies, b_copies = [], []
    weights, sums = None, None
    for t in range(STEPS - 1):
        low_mid[t].wait_recv()
        if t == 3:
            for copy in a_copies:
                copy.wait_recv()
            acc = mom_a[0]
            for index in range(1, probes):
                acc = acc + mom_a[index]
            mom_b[s] = acc
            for off in range(1, spaces):
                b_copies.append(send(
                    mom_b.at[s], mom_b.at[s], mb_send.at[off], mb_recv.at[off],
                    {"space": lax.rem(s + off, spaces)},
                ))
        step(t, 1)
        step(t + 1, first)
        high_mid[t].wait_recv()
        step(t, high)
        step(t + 1, last)
        if t == 2:
            moment(7, 3, 4)
            moment(8, 4, 4)
            for off in range(1, probes):
                a_copies.append(send(
                    mom_a.at[p], mom_a.at[p], ma_send.at[off], ma_recv.at[off],
                    {"probe": lax.rem(p + off, probes)},
                ))
        if t + 2 < STEPS:
            step(t + 2, middle)
        if t + 3 < STEPS - 1:
            send_middle(t + 3)

        if t < 2:
            moment(2 * t + 3, t + 1, t + 2)
            moment(2 * t + 4, t + 2, t + 2)
        if t < STEPS - 2:
            products(t + 1)
        if t == STEPS - 3:
            for n in (3, 4, 5):
                loads[n].wait()
            for copy in b_copies:
                copy.wait_recv()
            acc = mom_b[0]
            for index in range(1, spaces):
                acc = acc + mom_b[index]
            raw = jnp.sum(acc, axis=1, keepdims=True) / total_sites
            base = (raw[0:1], raw[1:2])
            moments = list(base)
            for n in range(2, STEPS + 1):
                moments.append(2.0 * raw[n:n + 1] - base[n % 2])
            points = target.shape[1]
            spectrum = jnp.zeros((1, points), jnp.float32)
            for n in range(STEPS + 1):
                spectrum = spectrum + scaled[n:n + 1, 0:1] * moments[n] * table[n:n + 1, :]
            misfit = spectrum - target[...]
            weights = []
            for n in range(STEPS + 1):
                dot = jnp.sum(table[n:n + 1, :] * misfit, axis=1, keepdims=True)
                weights.append((2.0 / points) * scaled[n:n + 1, 0:1] * dot)
            sums = [None] * (STEPS + 1)
            for n in range(STEPS, 0, -1):
                sums[n] = weights[n] if n + 2 > STEPS else weights[n] + sums[n + 2]
            k = STEPS - 1
            for i in range(planes):
                here = v[k, first + i]
                du[1, k, i] = 2.0 * (here - following(here, 0))
                du[2, k, i] = 2.0 * (here - following(here, 1))
                if i < planes - 1:
                    du[0, k, i] = 2.0 * (here - v[k, first + i + 1])
            for d, i in every[:-1]:
                gradient(d, i, sums)
            rs_start(0)
            for i in range(planes):
                acc = weights[0] * v[0, first + i]
                for n in range(1, STEPS):
                    acc = acc + weights[n] * v[n, first + i]
                costate[0, i] = 2.0 * acc
            rs_finish(0)
            if levels > 1:
                rs_start(1)

    k = STEPS - 1
    du[0, k, planes - 1] = 2.0 * (v[k, last] - v[k, high])
    gradient(0, planes - 1, sums)
    d_copies = []
    for off in range(1, probes):
        other = lax.rem(p + off, probes)
        d_copies.append(send(
            g.at[early, rows_of(other)], direct.at[off - 1], d_send.at[off], d_recv.at[off],
            {"probe": other},
        ))
    for i in range(planes):
        costate[0, i] = costate[0, i] + 2.0 * weights[STEPS] * v[STEPS, first + i]
    costate_copy = pltpu.make_async_copy(costate, costate_out, load_sem.at[6])
    costate_copy.start()
    for level in range(1, levels):
        rs_finish(level)
        if level + 1 < levels:
            rs_start(level + 1)
    for d, i in every[:-1]:
        grad[d, i] = g[place(d, i), rows_of(p)]
    acc = g[early, rows_of(p)]
    for off in range(1, probes):
        d_copies[off - 1].wait_recv()
        acc = acc + direct[off - 1]
    grad[0, planes - 1] = acc
    grad_copy = pltpu.make_async_copy(grad, grad_out, load_sem.at[7])
    grad_copy.start()
    for copy in started:
        copy.wait_send()
    costate_copy.wait()
    grad_copy.wait()


def on_device(probe_amplitudes, site_mask, couplings, target):
    spaces, probes = lax.axis_size("space"), lax.axis_size("probe")
    planes, rows, lanes = site_mask.shape
    table, scaled = tables(target.shape[0])
    block = rows // probes
    levels = probes.bit_length() - 1
    f32 = jnp.float32
    total_sites = float(probes * spaces * planes * rows * lanes)
    dma = pltpu.SemaphoreType.DMA
    return pl.pallas_call(
        functools.partial(kernel, spaces, probes, total_sites),
        out_shape=(
            jax.ShapeDtypeStruct((1, planes, rows, lanes), f32),
            jax.ShapeDtypeStruct((3, planes, block, lanes), f32),
        ),
        in_specs=[pl.BlockSpec(memory_space=pltpu.HBM)] * 6,
        out_specs=(pl.BlockSpec(memory_space=pltpu.HBM),) * 2,
        scratch_shapes=[
            pltpu.VMEM((1, planes, rows, lanes), f32),
            pltpu.VMEM((3, planes, block, lanes), f32),
            pltpu.VMEM(probe_amplitudes.shape, f32),
            pltpu.VMEM(site_mask.shape, f32),
            pltpu.VMEM(couplings.shape, f32),
            pltpu.VMEM((1, target.shape[0]), f32),
            pltpu.VMEM(table.shape, f32),
            pltpu.VMEM(scaled.shape, f32),
            pltpu.VMEM((STEPS + 1, planes + 4, rows, lanes), f32),
            pltpu.VMEM((3, STEPS, planes, rows, lanes), f32),
            pltpu.VMEM((STEPS, 3 * planes, rows, lanes), f32),
            pltpu.VMEM((3 * planes, rows, lanes), f32),
            pltpu.VMEM((3, planes + 3, rows, lanes), f32),
            pltpu.VMEM((3, planes, rows, lanes), f32),
            pltpu.VMEM((2, 4, rows, lanes), f32),
            pltpu.VMEM((2, 4, rows, lanes), f32),
            pltpu.VMEM((probes, ROWS, LANES), f32),
            pltpu.VMEM((spaces, ROWS, LANES), f32),
            pltpu.VMEM((levels, probes // 2, 3 * planes - 1, block, lanes), f32),
            pltpu.VMEM((probes - 1, block, lanes), f32),
            dma((8,)), dma((2,)), dma((2,)), dma((STEPS, 2)), dma((STEPS, 2)),
            dma((2, 2)), dma((2, 2)), dma((2, 2)), dma((2, 2)),
            dma((probes,)), dma((probes,)), dma((spaces,)), dma((spaces,)),
            dma((levels, probes // 2)), dma((levels, probes // 2)),
            dma((probes,)), dma((probes,)),
        ],
        compiler_params=pltpu.CompilerParams(
            collective_id=0, has_side_effects=True, vmem_limit_bytes=64 * 1024 * 1024
        ),
    )(probe_amplitudes, site_mask, couplings, target[None], table, scaled)


def solution(mesh):
    return jax.shard_map(
        on_device,
        mesh=mesh,
        in_specs=(
            P(("groups", "probe"), "space", None, None),
            P(("groups", "space"), None, None),
            P(None, ("groups", "space"), None, None),
            P("groups"),
        ),
        out_specs=(
            P(("groups", "probe"), "space", None, None),
            P(None, ("groups", "space"), "probe", None),
        ),
        check_vma=False,
    )
```

```python
import functools

import jax
import jax.numpy as jnp
import numpy as np
from jax import lax
from jax.experimental import pallas as pl
from jax.experimental.pallas import tpu as pltpu
from jax.sharding import PartitionSpec as P

STEPS = 8
SCALE = 10.0
MESH = pl.DeviceIdType.MESH
ROWS = 16
LANES = 128


def tables(points):
    count = STEPS + 1
    order = np.arange(count)
    theta = np.pi * (np.arange(points) + 0.5) / points
    total = count + 1.0
    jackson = (
        (total - order) * np.cos(np.pi * order / total)
        + np.sin(np.pi * order / total) / np.tan(np.pi / total)
    ) / total
    table = np.zeros((ROWS, points), np.float32)
    table[:count] = np.cos(order[:, None] * theta[None, :])
    scaled = np.zeros((ROWS, LANES), np.float32)
    scaled[:count] = (np.where(order > 0, 2.0, 1.0) * jackson)[:, None]
    return table, scaled


def following(x, axis):
    return pltpu.roll(x, x.shape[axis] - 1, axis)


def preceding(x, axis):
    return pltpu.roll(x, 1, axis)


def flipped(index, bit):
    return index + bit - 2 * bit * lax.rem(lax.div(index, bit), 2)


def kernel(
    spaces, probes, total_sites,
    amp_in, mask_in, coup_in, target_in, table_in, scaled_in,
    costate_out, grad_out,
    costate, grad, amp, mask, coup, target, table, scaled,
    v, du, q, g, bond, pair, give, got, mom_a, mom_b, recv, direct,
    load_sem, edge_send, edge_recv, mid_send, mid_recv,
    give_send, give_recv, pass_send, pass_recv,
    ma_send, ma_recv, mb_send, mb_recv, rs_send, rs_recv, d_send, d_recv,
):
    planes, rows, _ = mask.shape
    first, last, high = 2, planes + 1, planes + 2
    middle = 3
    block = rows // probes
    half = rows // 2
    s = lax.axis_index("space")
    p = lax.axis_index("probe")
    after, before = lax.rem(s + 1, spaces), lax.rem(s + spaces - 1, spaces)
    twin = flipped(p, 1)

    barrier = pltpu.get_barrier_semaphore()
    for off in range(1, spaces):
        pl.semaphore_signal(
            barrier, inc=1, device_id={"space": lax.rem(s + off, spaces)}, device_id_type=MESH
        )
    for off in range(1, probes):
        pl.semaphore_signal(
            barrier, inc=1, device_id={"probe": lax.rem(p + off, probes)}, device_id_type=MESH
        )

    loads = []
    for n, (src, dst) in enumerate([
        (mask_in, mask), (amp_in, amp), (coup_in, coup),
        (target_in, target), (table_in, table), (scaled_in, scaled),
    ]):
        loads.append(pltpu.make_async_copy(src, dst, load_sem.at[n]))
        loads[-1].start()

    started = []

    def send(src, dst, send_sem, recv_sem, where):
        copy = pltpu.make_async_remote_copy(
            src_ref=src, dst_ref=dst, send_sem=send_sem, recv_sem=recv_sem,
            device_id=where, device_id_type=MESH,
        )
        copy.start()
        started.append(copy)
        return copy

    low_mid, high_mid = {}, {}

    def send_middle(k):
        low_mid[k] = send(
            v.at[k, middle], v.at[k, 0], mid_send.at[k, 0], mid_recv.at[k, 0], {"space": after}
        )
        high_mid[k] = send(
            v.at[k, middle], v.at[k, high + 1], mid_send.at[k, 1], mid_recv.at[k, 1], {"space": before}
        )

    own_half = pl.ds(pl.multiple_of(lax.rem(p, 2) * half, half), half)

    def send_bonds(group, start, size):
        out = []
        for side, where in ((0, after), (1, before)):
            out.append(send(
                give.at[side, pl.ds(start, size), own_half],
                got.at[side, pl.ds(start, size), own_half],
                give_send.at[group, side], give_recv.at[group, side], {"space": where},
            ))
        return out

    def pass_bonds(group, start, size, copies):
        out = []
        for side in (0, 1):
            copies[side].wait_recv()
            out.append(send(
                got.at[side, pl.ds(start, size), own_half],
                got.at[side, pl.ds(start, size), own_half],
                pass_send.at[group, side], pass_recv.at[group, side], {"probe": twin},
            ))
        return out

    for n in (0, 1):
        loads[n].wait()
    for i in range(planes):
        v[0, first + i] = amp[0, i] * mask[i]
    pl.semaphore_wait(barrier, spaces + probes - 2)
    edge_low = send(v.at[0, last], v.at[0, 1], edge_send.at[0], edge_recv.at[0], {"space": after})
    edge_high = send(v.at[0, first], v.at[0, high], edge_send.at[1], edge_recv.at[1], {"space": before})
    loads[2].wait()
    give[0, 0] = (2.0 / SCALE) * (coup[0, planes - 1] * mask[planes - 1])
    give[1, 0] = mask[0]
    near = send_bonds(0, 0, 1)
    send_middle(0)

    for i in range(planes):
        m = mask[i]
        tenth = m * (1.0 / SCALE)
        if i < planes - 1:
            pair[0, i] = tenth * mask[i + 1]
            bond[0, first + i] = 2.0 * coup[0, i] * pair[0, i]
        pair[1, i] = tenth * following(m, 0)
        pair[2, i] = tenth * following(m, 1)
        for d in (1, 2):
            bond[d, first + i] = 2.0 * coup[d, i] * pair[d, i]
    give[0, 1] = bond[0, last - 1]
    give[1, 1] = bond[0, first]
    for d in (1, 2):
        give[0, d + 1] = bond[d, last]
        give[1, d + 1] = bond[d, first]
    far = send_bonds(1, 1, 3)

    def strength(d, j):
        if d == 0 and j == 0:
            return got[0, 1]
        if d == 0 and j == high:
            return got[1, 1]
        if d > 0 and j == 1:
            return got[0, d + 1]
        if d > 0 and j == high:
            return got[1, d + 1]
        return bond[d, j]

    def factor(k):
        return 1.0 if k == 0 else 2.0

    def step(k, j):
        here = v[k, j]
        d0 = here - v[k, j + 1]
        d1 = here - following(here, 0)
        d2 = here - following(here, 1)
        f1 = strength(1, j) * d1
        f2 = strength(2, j) * d2
        inside = (f1 - preceding(f1, 0)) + (f2 - preceding(f2, 1))
        inside = inside + strength(0, j) * d0
        inside = inside + strength(0, j - 1) * (here - v[k, j - 1])
        if k == 0:
            v[1, j] = 0.5 * inside - here
        else:
            v[k + 1, j] = inside - 2.0 * here - v[k - 1, j]
        if first <= j <= last and k < STEPS - 1:
            du[0, k, j - first] = factor(k) * d0
            du[1, k, j - first] = factor(k) * d1
            du[2, k, j - first] = factor(k) * d2

    def moment(n, i, j):
        acc = v[i, first] * v[j, first]
        for plane in range(first + 1, last + 1):
            acc = acc + v[i, plane] * v[j, plane]
        row = jnp.sum(acc, axis=0, keepdims=True)
        part = row[:, :LANES]
        for start in range(LANES, row.shape[1], LANES):
            part = part + row[:, start:start + LANES]
        mom_a[p, pl.ds(n, 1), :] = part

    def product(n, d, i):
        acc = None
        for a in range(n // 2 + 1):
            term = du[d, a, i] * du[d, n - a, i]
            if a != n - a:
                term = 2.0 * term
            acc = term if acc is None else acc + term
        return acc

    def place(d, i):
        if d == 0:
            return 2 * planes + i
        return (d - 1) * planes + i

    every = [(d, i) for d in (1, 2, 0) for i in range(planes)]
    early = 3 * planes - 1

    def products(n):
        for d, i in every:
            q[n, place(d, i)] = product(n, d, i)

    def gradient_before(d, i, sums):
        acc = sums[1] * q[0, place(d, i)]
        for n in range(1, STEPS - 2):
            acc = acc + sums[n + 1] * q[n, place(d, i)]
        g[place(d, i)] = acc

    def gradient(d, i, sums):
        acc = g[place(d, i)]
        for n in (STEPS - 2, STEPS - 1):
            acc = acc + sums[n + 1] * product(n, d, i)
        g[place(d, i)] = pair[d, i] * acc

    def rows_of(index):
        return pl.ds(pl.multiple_of(index * block, block), block)

    levels = probes.bit_length() - 1
    parts = ((0, early // 2), (early // 2, early))
    rs_copies = {}

    def rs_start(level, part):
        bit = 1 << level
        other = flipped(p, bit)
        start, stop = parts[part]
        rs_copies[level, part] = []
        for j in range(probes // (2 * bit)):
            index = lax.rem(other, 2 * bit) + j * 2 * bit
            rs_copies[level, part].append(send(
                g.at[pl.ds(start, stop - start), rows_of(index)],
                recv.at[level, j, pl.ds(start, stop - start)],
                rs_send.at[level, j, part], rs_recv.at[level, j, part], {"probe": other},
            ))

    def rs_finish(level, part):
        bit = 1 << level
        start, stop = parts[part]
        here = pl.ds(start, stop - start)
        for j, copy in enumerate(rs_copies[level, part]):
            copy.wait_recv()
            index = lax.rem(p, 2 * bit) + j * 2 * bit
            g[here, rows_of(index)] = g[here, rows_of(index)] + recv[level, j, here]

    step(0, middle)
    send_middle(1)
    near = pass_bonds(0, 0, 1, near)
    mom_a[p, pl.ds(8, 8), :] = jnp.zeros((8, LANES), jnp.float32)
    moment(0, 0, 0)
    for copy in near:
        copy.wait_recv()
    bond[0, 1] = got[0, 0] * mask[0]
    pair[0, planes - 1] = mask[planes - 1] * (1.0 / SCALE) * got[1, 0]
    bond[0, last] = 2.0 * coup[0, planes - 1] * pair[0, planes - 1]
    edge_low.wait_recv()
    step(0, first)
    edge_high.wait_recv()
    step(0, last)
    step(1, middle)
    send_middle(2)
    far = pass_bonds(1, 1, 3, far)
    moment(1, 0, 1)
    moment(2, 1, 1)
    products(0)
    for copy in far:
        copy.wait_recv()

    a_copies, b_copies = [], []
    weights, sums = None, None
    for t in range(STEPS - 2):
        low_mid[t].wait_recv()
        if t == 3:
            for copy in a_copies:
                copy.wait_recv()
            acc = mom_a[0]
            for index in range(1, probes):
                acc = acc + mom_a[index]
            mom_b[s] = acc
            for off in range(1, spaces):
                b_copies.append(send(
                    mom_b.at[s], mom_b.at[s], mb_send.at[off], mb_recv.at[off],
                    {"space": lax.rem(s + off, spaces)},
                ))
        step(t, 1)
        step(t + 1, first)
        high_mid[t].wait_recv()
        step(t, high)
        step(t + 1, last)
        if t == 2:
            moment(7, 3, 4)
            moment(8, 4, 4)
            for off in range(1, probes):
                a_copies.append(send(
                    mom_a.at[p], mom_a.at[p], ma_send.at[off], ma_recv.at[off],
                    {"probe": lax.rem(p + off, probes)},
                ))
        if t + 2 < STEPS - 1:
            step(t + 2, middle)
        if t + 3 < STEPS - 1:
            send_middle(t + 3)

        if t < 2:
            moment(2 * t + 3, t + 1, t + 2)
            moment(2 * t + 4, t + 2, t + 2)
        if t < STEPS - 3:
            products(t + 1)
        if t == STEPS - 4:
            for n in (3, 4, 5):
                loads[n].wait()
            for copy in b_copies:
                copy.wait_recv()
            acc = mom_b[0]
            for index in range(1, spaces):
                acc = acc + mom_b[index]
            raw = jnp.sum(acc, axis=1, keepdims=True) / total_sites
            base = (raw[0:1], raw[1:2])
            moments = list(base)
            for n in range(2, STEPS + 1):
                moments.append(2.0 * raw[n:n + 1] - base[n % 2])
            points = target.shape[1]
            spectrum = jnp.zeros((1, points), jnp.float32)
            for n in range(STEPS + 1):
                spectrum = spectrum + scaled[n:n + 1, 0:1] * moments[n] * table[n:n + 1, :]
            misfit = spectrum - target[...]
            weights = []
            for n in range(STEPS + 1):
                dot = jnp.sum(table[n:n + 1, :] * misfit, axis=1, keepdims=True)
                weights.append((2.0 / points) * scaled[n:n + 1, 0:1] * dot)
            sums = [None] * (STEPS + 1)
            for n in range(STEPS, 0, -1):
                sums[n] = weights[n] if n + 2 > STEPS else weights[n] + sums[n + 2]
            for d, i in every:
                gradient_before(d, i, sums)
        if t == STEPS - 3:
            k = STEPS - 1
            for i in range(planes):
                here = v[k, first + i]
                du[1, k, i] = 2.0 * (here - following(here, 0))
                du[2, k, i] = 2.0 * (here - following(here, 1))
                if i < planes - 1:
                    du[0, k, i] = 2.0 * (here - v[k, first + i + 1])
            for part, (start, stop) in enumerate(parts):
                for d, i in every[start:stop]:
                    gradient(d, i, sums)
                rs_start(0, part)
            step(t + 2, middle)
            for i in range(planes):
                acc = weights[0] * v[0, first + i]
                for n in range(1, STEPS):
                    acc = acc + weights[n] * v[n, first + i]
                costate[0, i] = acc
            for part in range(len(parts)):
                rs_finish(0, part)
                if levels > 1:
                    rs_start(1, part)

    k = STEPS - 1
    high_mid[k - 1].wait_recv()
    step(k - 1, high)
    du[0, k, planes - 1] = 2.0 * (v[k, last] - v[k, high])
    gradient(0, planes - 1, sums)
    d_copies = []
    for off in range(1, probes):
        other = lax.rem(p + off, probes)
        d_copies.append(send(
            g.at[early, rows_of(other)], direct.at[off - 1], d_send.at[off], d_recv.at[off],
            {"probe": other},
        ))
    step(k, last)
    low_mid[k - 1].wait_recv()
    step(k - 1, 1)
    step(k, first)
    for i in range(planes):
        costate[0, i] = costate[0, i] + weights[STEPS] * v[STEPS, first + i]
    costate_copy = pltpu.make_async_copy(costate, costate_out, load_sem.at[6])
    costate_copy.start()
    for level in range(1, levels):
        for part in range(len(parts)):
            rs_finish(level, part)
            if level + 1 < levels:
                rs_start(level + 1, part)
    for d, i in every[:-1]:
        grad[d, i] = g[place(d, i), rows_of(p)]
    acc = g[early, rows_of(p)]
    for off in range(1, probes):
        d_copies[off - 1].wait_recv()
        acc = acc + direct[off - 1]
    grad[0, planes - 1] = acc
    grad_copy = pltpu.make_async_copy(grad, grad_out, load_sem.at[7])
    grad_copy.start()
    for copy in started:
        copy.wait_send()
    costate_copy.wait()
    grad_copy.wait()


def on_device(probe_amplitudes, site_mask, couplings, target):
    spaces, probes = lax.axis_size("space"), lax.axis_size("probe")
    planes, rows, lanes = site_mask.shape
    table, scaled = tables(target.shape[0])
    block = rows // probes
    levels = probes.bit_length() - 1
    f32 = jnp.float32
    total_sites = float(probes * spaces * planes * rows * lanes)
    dma = pltpu.SemaphoreType.DMA
    costate, grad = pl.pallas_call(
        functools.partial(kernel, spaces, probes, total_sites),
        out_shape=(
            jax.ShapeDtypeStruct((1, planes, rows, lanes), f32),
            jax.ShapeDtypeStruct((3, planes, block, lanes), f32),
        ),
        in_specs=[pl.BlockSpec(memory_space=pltpu.HBM)] * 6,
        out_specs=(pl.BlockSpec(memory_space=pltpu.HBM),) * 2,
        scratch_shapes=[
            pltpu.VMEM((1, planes, rows, lanes), f32),
            pltpu.VMEM((3, planes, block, lanes), f32),
            pltpu.VMEM(probe_amplitudes.shape, f32),
            pltpu.VMEM(site_mask.shape, f32),
            pltpu.VMEM(couplings.shape, f32),
            pltpu.VMEM((1, target.shape[0]), f32),
            pltpu.VMEM(table.shape, f32),
            pltpu.VMEM(scaled.shape, f32),
            pltpu.VMEM((STEPS + 1, planes + 4, rows, lanes), f32),
            pltpu.VMEM((3, STEPS, planes, rows, lanes), f32),
            pltpu.VMEM((STEPS, 3 * planes, rows, lanes), f32),
            pltpu.VMEM((3 * planes, rows, lanes), f32),
            pltpu.VMEM((3, planes + 3, rows, lanes), f32),
            pltpu.VMEM((3, planes, rows, lanes), f32),
            pltpu.VMEM((2, 4, rows, lanes), f32),
            pltpu.VMEM((2, 4, rows, lanes), f32),
            pltpu.VMEM((probes, ROWS, LANES), f32),
            pltpu.VMEM((spaces, ROWS, LANES), f32),
            pltpu.VMEM((levels, probes // 2, 3 * planes - 1, block, lanes), f32),
            pltpu.VMEM((probes - 1, block, lanes), f32),
            dma((8,)), dma((2,)), dma((2,)), dma((STEPS, 2)), dma((STEPS, 2)),
            dma((2, 2)), dma((2, 2)), dma((2, 2)), dma((2, 2)),
            dma((probes,)), dma((probes,)), dma((spaces,)), dma((spaces,)),
            dma((levels, probes // 2, 2)), dma((levels, probes // 2, 2)),
            dma((probes,)), dma((probes,)),
        ],
        compiler_params=pltpu.CompilerParams(
            collective_id=0, has_side_effects=True, vmem_limit_bytes=64 * 1024 * 1024
        ),
    )(probe_amplitudes, site_mask, couplings, target[None], table, scaled)
    return 2.0 * costate, grad


def solution(mesh):
    return jax.shard_map(
        on_device,
        mesh=mesh,
        in_specs=(
            P(("groups", "probe"), "space", None, None),
            P(("groups", "space"), None, None),
            P(None, ("groups", "space"), None, None),
            P("groups"),
        ),
        out_specs=(
            P(("groups", "probe"), "space", None, None),
            P(None, ("groups", "space"), "probe", None),
        ),
        check_vma=False,
    )
```

```python
import functools

import jax
import jax.numpy as jnp
import numpy as np
from jax import lax
from jax.experimental import pallas as pl
from jax.experimental.pallas import tpu as pltpu
from jax.sharding import PartitionSpec as P

STEPS = 8
SCALE = 10.0
MESH = pl.DeviceIdType.MESH
ROWS = 16
LANES = 128


def tables(points):
    count = STEPS + 1
    order = np.arange(count)
    theta = np.pi * (np.arange(points) + 0.5) / points
    total = count + 1.0
    jackson = (
        (total - order) * np.cos(np.pi * order / total)
        + np.sin(np.pi * order / total) / np.tan(np.pi / total)
    ) / total
    table = np.zeros((ROWS, points), np.float32)
    table[:count] = np.cos(order[:, None] * theta[None, :])
    scaled = np.zeros((ROWS, LANES), np.float32)
    scaled[:count] = (np.where(order > 0, 2.0, 1.0) * jackson)[:, None]
    return table, scaled


def following(x, axis):
    return pltpu.roll(x, x.shape[axis] - 1, axis)


def preceding(x, axis):
    return pltpu.roll(x, 1, axis)


def flipped(index, bit):
    return index + bit - 2 * bit * lax.rem(lax.div(index, bit), 2)


def kernel(
    spaces, probes, total_sites,
    amp_in, mask_in, coup_in, target_in, table_in, scaled_in,
    costate, grad,
    amp, mask, coup, target, table, scaled,
    v, du, q, g, bond, pair, give, got, mom_a, mom_b, recv, direct,
    load_sem, edge_send, edge_recv, mid_send, mid_recv,
    give_send, give_recv, pass_send, pass_recv,
    ma_send, ma_recv, mb_send, mb_recv, rs_send, rs_recv, d_send, d_recv,
):
    planes, rows, _ = mask.shape
    first, last, high = 2, planes + 1, planes + 2
    middle = 3
    block = rows // probes
    half = rows // 2
    s = lax.axis_index("space")
    p = lax.axis_index("probe")
    after, before = lax.rem(s + 1, spaces), lax.rem(s + spaces - 1, spaces)
    twin = flipped(p, 1)

    barrier = pltpu.get_barrier_semaphore()
    for off in range(1, spaces):
        pl.semaphore_signal(
            barrier, inc=1, device_id={"space": lax.rem(s + off, spaces)}, device_id_type=MESH
        )
    for off in range(1, probes):
        pl.semaphore_signal(
            barrier, inc=1, device_id={"probe": lax.rem(p + off, probes)}, device_id_type=MESH
        )

    loads = []
    for n, (src, dst) in enumerate([
        (mask_in, mask), (amp_in, amp), (coup_in, coup),
        (target_in, target), (table_in, table), (scaled_in, scaled),
    ]):
        loads.append(pltpu.make_async_copy(src, dst, load_sem.at[n]))
        loads[-1].start()

    started = []

    def send(src, dst, send_sem, recv_sem, where):
        copy = pltpu.make_async_remote_copy(
            src_ref=src, dst_ref=dst, send_sem=send_sem, recv_sem=recv_sem,
            device_id=where, device_id_type=MESH,
        )
        copy.start()
        started.append(copy)
        return copy

    low_mid, high_mid = {}, {}

    def send_middle(k):
        low_mid[k] = send(
            v.at[k, middle], v.at[k, 0], mid_send.at[k, 0], mid_recv.at[k, 0], {"space": after}
        )
        high_mid[k] = send(
            v.at[k, middle], v.at[k, high + 1], mid_send.at[k, 1], mid_recv.at[k, 1], {"space": before}
        )

    own_half = pl.ds(pl.multiple_of(lax.rem(p, 2) * half, half), half)

    levels = probes.bit_length() - 1
    turned = sum(lax.rem(lax.div(p, 1 << i), 2) * (1 << (levels - 1 - i)) for i in range(levels))

    def shared_rows(level):
        size = block << level
        return pl.ds(pl.multiple_of(lax.div(turned, 1 << level) * size, size), size)

    def send_bonds(group, start, size, rows):
        out = []
        for side, where in ((0, after), (1, before)):
            out.append(send(
                give.at[side, pl.ds(start, size), rows],
                got.at[side, pl.ds(start, size), rows],
                give_send.at[group, side], give_recv.at[group, side], {"space": where},
            ))
        return out

    def pass_bonds(slot, start, size, rows, where, copies):
        out = []
        for side in (0, 1):
            copies[side].wait_recv()
            out.append(send(
                got.at[side, pl.ds(start, size), rows],
                got.at[side, pl.ds(start, size), rows],
                pass_send.at[slot, side], pass_recv.at[slot, side], {"probe": where},
            ))
        return out

    def pass_far(level, copies):
        return pass_bonds(
            1 + level, 1, 3, shared_rows(level), flipped(p, probes >> (level + 1)), copies
        )

    for n in (0, 1):
        loads[n].wait()
    for i in range(planes):
        v[0, first + i] = amp[0, i] * mask[i]
    pl.semaphore_wait(barrier, spaces + probes - 2)
    edge_low = send(v.at[0, last], v.at[0, 1], edge_send.at[0], edge_recv.at[0], {"space": after})
    edge_high = send(v.at[0, first], v.at[0, high], edge_send.at[1], edge_recv.at[1], {"space": before})
    loads[2].wait()

    def across(d, i):
        pair[d, i] = mask[i] * (1.0 / SCALE) * following(mask[i], d - 1)
        bond[d, first + i] = 2.0 * coup[d, i] * pair[d, i]

    for i in range(planes - 1):
        pair[0, i] = mask[i] * (1.0 / SCALE) * mask[i + 1]
        bond[0, first + i] = 2.0 * coup[0, i] * pair[0, i]
    give[0, 1] = bond[0, last - 1]
    give[1, 1] = bond[0, first]
    for d in (1, 2):
        for i in (0, planes - 1):
            across(d, i)
        give[0, d + 1] = bond[d, last]
        give[1, d + 1] = bond[d, first]
    far = send_bonds(1, 1, 3, shared_rows(0))
    give[0, 0] = (2.0 / SCALE) * (coup[0, planes - 1] * mask[planes - 1])
    give[1, 0] = mask[0]
    near = send_bonds(0, 0, 1, own_half)
    send_middle(0)
    for d in (1, 2):
        for i in range(1, planes - 1):
            across(d, i)

    def strength(d, j):
        if d == 0 and j == 0:
            return got[0, 1]
        if d == 0 and j == high:
            return got[1, 1]
        if d > 0 and j == 1:
            return got[0, d + 1]
        if d > 0 and j == high:
            return got[1, d + 1]
        return bond[d, j]

    def factor(k):
        return 1.0 if k == 0 else 2.0

    def step(k, j):
        here = v[k, j]
        d0 = here - v[k, j + 1]
        d1 = here - following(here, 0)
        d2 = here - following(here, 1)
        f1 = strength(1, j) * d1
        f2 = strength(2, j) * d2
        inside = (f1 - preceding(f1, 0)) + (f2 - preceding(f2, 1))
        inside = inside + strength(0, j) * d0
        inside = inside + strength(0, j - 1) * (here - v[k, j - 1])
        if k == 0:
            v[1, j] = 0.5 * inside - here
        else:
            v[k + 1, j] = inside - 2.0 * here - v[k - 1, j]
        if first <= j <= last and k < STEPS - 1:
            du[0, k, j - first] = factor(k) * d0
            du[1, k, j - first] = factor(k) * d1
            du[2, k, j - first] = factor(k) * d2

    def moment(n, i, j):
        acc = v[i, first] * v[j, first]
        for plane in range(first + 1, last + 1):
            acc = acc + v[i, plane] * v[j, plane]
        row = jnp.sum(acc, axis=0, keepdims=True)
        part = row[:, :LANES]
        for start in range(LANES, row.shape[1], LANES):
            part = part + row[:, start:start + LANES]
        mom_a[p, pl.ds(n, 1), :] = part

    def product(n, d, i):
        acc = None
        for a in range(n // 2 + 1):
            term = du[d, a, i] * du[d, n - a, i]
            if a != n - a:
                term = 2.0 * term
            acc = term if acc is None else acc + term
        return acc

    def place(d, i):
        if d == 0:
            return 2 * planes + i
        return (d - 1) * planes + i

    every = [(d, i) for d in (1, 2, 0) for i in range(planes)]
    early = 3 * planes - 1

    def products(n):
        for d, i in every:
            q[n, place(d, i)] = product(n, d, i)

    def gradient_before(d, i, sums):
        acc = sums[1] * q[0, place(d, i)]
        for n in range(1, STEPS - 2):
            acc = acc + sums[n + 1] * q[n, place(d, i)]
        g[place(d, i)] = acc

    def gradient(d, i, sums):
        acc = g[place(d, i)]
        for n in (STEPS - 2, STEPS - 1):
            acc = acc + sums[n + 1] * product(n, d, i)
        g[place(d, i)] = pair[d, i] * acc

    def rows_of(index):
        return pl.ds(pl.multiple_of(index * block, block), block)

    parts = ((0, early // 2), (early // 2, early))
    rs_copies = {}

    def rs_start(level, part):
        bit = 1 << level
        other = flipped(p, bit)
        start, stop = parts[part]
        rs_copies[level, part] = []
        for j in range(probes // (2 * bit)):
            index = lax.rem(other, 2 * bit) + j * 2 * bit
            rs_copies[level, part].append(send(
                g.at[pl.ds(start, stop - start), rows_of(index)],
                recv.at[level, j, pl.ds(start, stop - start)],
                rs_send.at[level, j, part], rs_recv.at[level, j, part], {"probe": other},
            ))

    def rs_finish(level, part):
        bit = 1 << level
        start, stop = parts[part]
        here = pl.ds(start, stop - start)
        for j, copy in enumerate(rs_copies[level, part]):
            copy.wait_recv()
            index = lax.rem(p, 2 * bit) + j * 2 * bit
            g[here, rows_of(index)] = g[here, rows_of(index)] + recv[level, j, here]

    step(0, middle)
    send_middle(1)
    far = pass_far(0, far)
    near = pass_bonds(0, 0, 1, own_half, twin, near)
    mom_a[p, pl.ds(8, 8), :] = jnp.zeros((8, LANES), jnp.float32)
    moment(0, 0, 0)
    for copy in near:
        copy.wait_recv()
    bond[0, 1] = got[0, 0] * mask[0]
    pair[0, planes - 1] = mask[planes - 1] * (1.0 / SCALE) * got[1, 0]
    bond[0, last] = 2.0 * coup[0, planes - 1] * pair[0, planes - 1]
    edge_low.wait_recv()
    step(0, first)
    edge_high.wait_recv()
    step(0, last)
    step(1, middle)
    send_middle(2)
    for level in range(1, levels):
        far = pass_far(level, far)
    moment(1, 0, 1)
    moment(2, 1, 1)
    products(0)
    for copy in far:
        copy.wait_recv()

    a_copies, b_copies = [], []
    weights, sums = None, None
    for t in range(STEPS - 2):
        low_mid[t].wait_recv()
        if t == 3:
            for copy in a_copies:
                copy.wait_recv()
            acc = mom_a[0]
            for index in range(1, probes):
                acc = acc + mom_a[index]
            mom_b[s] = acc
            for off in range(1, spaces):
                b_copies.append(send(
                    mom_b.at[s], mom_b.at[s], mb_send.at[off], mb_recv.at[off],
                    {"space": lax.rem(s + off, spaces)},
                ))
        step(t, 1)
        step(t + 1, first)
        high_mid[t].wait_recv()
        step(t, high)
        step(t + 1, last)
        if t == 2:
            moment(7, 3, 4)
            moment(8, 4, 4)
            for off in range(1, probes):
                a_copies.append(send(
                    mom_a.at[p], mom_a.at[p], ma_send.at[off], ma_recv.at[off],
                    {"probe": lax.rem(p + off, probes)},
                ))
        if t + 2 < STEPS - 1:
            step(t + 2, middle)
        if t + 3 < STEPS - 1:
            send_middle(t + 3)

        if t < 2:
            moment(2 * t + 3, t + 1, t + 2)
            moment(2 * t + 4, t + 2, t + 2)
        if t < STEPS - 3:
            products(t + 1)
        if t == STEPS - 4:
            for n in (3, 4, 5):
                loads[n].wait()
            for copy in b_copies:
                copy.wait_recv()
            acc = mom_b[0]
            for index in range(1, spaces):
                acc = acc + mom_b[index]
            raw = jnp.sum(acc, axis=1, keepdims=True) / total_sites
            base = (raw[0:1], raw[1:2])
            moments = list(base)
            for n in range(2, STEPS + 1):
                moments.append(2.0 * raw[n:n + 1] - base[n % 2])
            points = target.shape[1]
            spectrum = jnp.zeros((1, points), jnp.float32)
            for n in range(STEPS + 1):
                spectrum = spectrum + scaled[n:n + 1, 0:1] * moments[n] * table[n:n + 1, :]
            misfit = spectrum - target[...]
            weights = []
            for n in range(STEPS + 1):
                dot = jnp.sum(table[n:n + 1, :] * misfit, axis=1, keepdims=True)
                weights.append((2.0 / points) * scaled[n:n + 1, 0:1] * dot)
            sums = [None] * (STEPS + 1)
            for n in range(STEPS, 0, -1):
                sums[n] = weights[n] if n + 2 > STEPS else weights[n] + sums[n + 2]
            for d, i in every:
                gradient_before(d, i, sums)
        if t == STEPS - 3:
            k = STEPS - 1
            for i in range(planes):
                here = v[k, first + i]
                du[1, k, i] = 2.0 * (here - following(here, 0))
                du[2, k, i] = 2.0 * (here - following(here, 1))
                if i < planes - 1:
                    du[0, k, i] = 2.0 * (here - v[k, first + i + 1])
            for part, (start, stop) in enumerate(parts):
                for d, i in every[start:stop]:
                    gradient(d, i, sums)
                rs_start(0, part)
            step(t + 2, middle)
            for i in range(planes):
                acc = weights[0] * v[0, first + i]
                for n in range(1, STEPS):
                    acc = acc + weights[n] * v[n, first + i]
                costate[0, i] = 2.0 * acc
            for part in range(len(parts)):
                rs_finish(0, part)
                if levels > 1:
                    rs_start(1, part)

    k = STEPS - 1
    high_mid[k - 1].wait_recv()
    step(k - 1, high)
    du[0, k, planes - 1] = 2.0 * (v[k, last] - v[k, high])
    gradient(0, planes - 1, sums)
    d_copies = []
    for off in range(1, probes):
        other = lax.rem(p + off, probes)
        d_copies.append(send(
            g.at[early, rows_of(other)], direct.at[off - 1], d_send.at[off], d_recv.at[off],
            {"probe": other},
        ))
    step(k, last)
    low_mid[k - 1].wait_recv()
    step(k - 1, 1)
    step(k, first)
    for i in range(planes):
        costate[0, i] = costate[0, i] + 2.0 * weights[STEPS] * v[STEPS, first + i]
    for level in range(1, levels):
        for part in range(len(parts)):
            rs_finish(level, part)
            if level + 1 < levels:
                rs_start(level + 1, part)
    for d, i in every[:-1]:
        grad[d, i] = g[place(d, i), rows_of(p)]
    acc = g[early, rows_of(p)]
    for off in range(1, probes):
        d_copies[off - 1].wait_recv()
        acc = acc + direct[off - 1]
    grad[0, planes - 1] = acc
    for copy in started:
        copy.wait_send()


def on_device(probe_amplitudes, site_mask, couplings, target):
    spaces, probes = lax.axis_size("space"), lax.axis_size("probe")
    planes, rows, lanes = site_mask.shape
    table, scaled = tables(target.shape[0])
    block = rows // probes
    levels = probes.bit_length() - 1
    f32 = jnp.float32
    total_sites = float(probes * spaces * planes * rows * lanes)
    dma = pltpu.SemaphoreType.DMA
    costate, grad = pl.pallas_call(
        functools.partial(kernel, spaces, probes, total_sites),
        out_shape=(
            pltpu.VMEM((1, planes, rows, lanes), f32),
            pltpu.VMEM((3, planes, block, lanes), f32),
        ),
        in_specs=[pl.BlockSpec(memory_space=pltpu.HBM)] * 6,
        out_specs=(pl.BlockSpec(memory_space=pltpu.VMEM),) * 2,
        scratch_shapes=[
            pltpu.VMEM(probe_amplitudes.shape, f32),
            pltpu.VMEM(site_mask.shape, f32),
            pltpu.VMEM(couplings.shape, f32),
            pltpu.VMEM((1, target.shape[0]), f32),
            pltpu.VMEM(table.shape, f32),
            pltpu.VMEM(scaled.shape, f32),
            pltpu.VMEM((STEPS + 1, planes + 4, rows, lanes), f32),
            pltpu.VMEM((3, STEPS, planes, rows, lanes), f32),
            pltpu.VMEM((STEPS, 3 * planes, rows, lanes), f32),
            pltpu.VMEM((3 * planes, rows, lanes), f32),
            pltpu.VMEM((3, planes + 3, rows, lanes), f32),
            pltpu.VMEM((3, planes, rows, lanes), f32),
            pltpu.VMEM((2, 4, rows, lanes), f32),
            pltpu.VMEM((2, 4, rows, lanes), f32),
            pltpu.VMEM((probes, ROWS, LANES), f32),
            pltpu.VMEM((spaces, ROWS, LANES), f32),
            pltpu.VMEM((levels, probes // 2, 3 * planes - 1, block, lanes), f32),
            pltpu.VMEM((probes - 1, block, lanes), f32),
            dma((6,)), dma((2,)), dma((2,)), dma((STEPS, 2)), dma((STEPS, 2)),
            dma((2, 2)), dma((2, 2)), dma((1 + levels, 2)), dma((1 + levels, 2)),
            dma((probes,)), dma((probes,)), dma((spaces,)), dma((spaces,)),
            dma((levels, probes // 2, 2)), dma((levels, probes // 2, 2)),
            dma((probes,)), dma((probes,)),
        ],
        compiler_params=pltpu.CompilerParams(
            collective_id=0, has_side_effects=True, vmem_limit_bytes=63 * 1024 * 1024
        ),
    )(probe_amplitudes, site_mask, couplings, target[None], table, scaled)
    return costate, grad


def solution(mesh):
    return jax.shard_map(
        on_device,
        mesh=mesh,
        in_specs=(
            P(("groups", "probe"), "space", None, None),
            P(("groups", "space"), None, None),
            P(None, ("groups", "space"), None, None),
            P("groups"),
        ),
        out_specs=(
            P(("groups", "probe"), "space", None, None),
            P(None, ("groups", "space"), "probe", None),
        ),
        check_vma=False,
    )
```

```python
import functools

import jax
import jax.numpy as jnp
import numpy as np
from jax import lax
from jax.experimental import pallas as pl
from jax.experimental.pallas import tpu as pltpu
from jax.sharding import PartitionSpec as P

STEPS = 8
SCALE = 10.0
MESH = pl.DeviceIdType.MESH
ROWS = 16
LANES = 128


def tables(points):
    count = STEPS + 1
    order = np.arange(count)
    theta = np.pi * (np.arange(points) + 0.5) / points
    total = count + 1.0
    jackson = (
        (total - order) * np.cos(np.pi * order / total)
        + np.sin(np.pi * order / total) / np.tan(np.pi / total)
    ) / total
    table = np.zeros((ROWS, points), np.float32)
    table[:count] = np.cos(order[:, None] * theta[None, :])
    scaled = np.zeros((ROWS, LANES), np.float32)
    scaled[:count] = (np.where(order > 0, 2.0, 1.0) * jackson)[:, None]
    return table, scaled


def following(x, axis):
    return pltpu.roll(x, x.shape[axis] - 1, axis)


def preceding(x, axis):
    return pltpu.roll(x, 1, axis)


def flipped(index, bit):
    return index + bit - 2 * bit * lax.rem(lax.div(index, bit), 2)


def kernel(
    spaces, probes, total_sites,
    amp_in, mask_in, coup_in, target_in, table_in, scaled_in,
    costate, grad,
    amp, mask, coup, target, table, scaled,
    v, du, q, g, bond, pair, give, got, mom_a, mom_b, recv, direct,
    load_sem, edge_send, edge_recv, mid_send, mid_recv,
    give_send, give_recv, pass_send, pass_recv,
    ma_send, ma_recv, mb_send, mb_recv, rs_send, rs_recv, d_send, d_recv,
):
    planes, rows, _ = mask.shape
    first, last, high = 2, planes + 1, planes + 2
    middle = 3
    block = rows // probes
    half = rows // 2
    s = lax.axis_index("space")
    p = lax.axis_index("probe")
    after, before = lax.rem(s + 1, spaces), lax.rem(s + spaces - 1, spaces)
    twin = flipped(p, 1)

    barrier = pltpu.get_barrier_semaphore()
    for off in [1, spaces - 1, *range(2, spaces - 1)]:
        pl.semaphore_signal(
            barrier, inc=1, device_id={"space": lax.rem(s + off, spaces)}, device_id_type=MESH
        )
    for off in range(1, probes):
        pl.semaphore_signal(
            barrier, inc=1, device_id={"probe": lax.rem(p + off, probes)}, device_id_type=MESH
        )

    loads = []
    for n, (src, dst) in enumerate([
        (mask_in, mask), (amp_in, amp), (coup_in, coup),
        (target_in, target), (table_in, table), (scaled_in, scaled),
    ]):
        loads.append(pltpu.make_async_copy(src, dst, load_sem.at[n]))
        loads[-1].start()

    started = []

    def send(src, dst, send_sem, recv_sem, where):
        copy = pltpu.make_async_remote_copy(
            src_ref=src, dst_ref=dst, send_sem=send_sem, recv_sem=recv_sem,
            device_id=where, device_id_type=MESH,
        )
        copy.start()
        started.append(copy)
        return copy

    low_mid, high_mid = {}, {}

    def send_middle(k):
        low_mid[k] = send(
            v.at[k, middle], v.at[k, 0], mid_send.at[k, 0], mid_recv.at[k, 0], {"space": after}
        )
        high_mid[k] = send(
            v.at[k, middle], v.at[k, high + 1], mid_send.at[k, 1], mid_recv.at[k, 1], {"space": before}
        )

    own_half = pl.ds(pl.multiple_of(lax.rem(p, 2) * half, half), half)

    levels = probes.bit_length() - 1
    turned = sum(lax.rem(lax.div(p, 1 << i), 2) * (1 << (levels - 1 - i)) for i in range(levels))

    def shared_rows(level):
        size = block << level
        return pl.ds(pl.multiple_of(lax.div(turned, 1 << level) * size, size), size)

    def send_bonds(group, start, size, rows):
        out = []
        for side, where in ((0, after), (1, before)):
            out.append(send(
                give.at[side, pl.ds(start, size), rows],
                got.at[side, pl.ds(start, size), rows],
                give_send.at[group, side], give_recv.at[group, side], {"space": where},
            ))
        return out

    def pass_bonds(slot, start, size, rows, where, copies):
        out = []
        for side in (0, 1):
            copies[side].wait_recv()
            out.append(send(
                got.at[side, pl.ds(start, size), rows],
                got.at[side, pl.ds(start, size), rows],
                pass_send.at[slot, side], pass_recv.at[slot, side], {"probe": where},
            ))
        return out

    def pass_far(level, copies):
        return pass_bonds(
            1 + level, 1, 3, shared_rows(level), flipped(p, probes >> (level + 1)), copies
        )

    for n in (0, 1):
        loads[n].wait()
    for i in range(planes):
        v[0, first + i] = amp[0, i] * mask[i]
    pl.semaphore_wait(barrier, spaces + probes - 2)
    edge_low = send(v.at[0, last], v.at[0, 1], edge_send.at[0], edge_recv.at[0], {"space": after})
    edge_high = send(v.at[0, first], v.at[0, high], edge_send.at[1], edge_recv.at[1], {"space": before})
    loads[2].wait()

    def across(d, i):
        pair[d, i] = mask[i] * (1.0 / SCALE) * following(mask[i], d - 1)
        bond[d, first + i] = 2.0 * coup[d, i] * pair[d, i]

    for i in range(planes - 1):
        pair[0, i] = mask[i] * (1.0 / SCALE) * mask[i + 1]
        bond[0, first + i] = 2.0 * coup[0, i] * pair[0, i]
    give[0, 1] = bond[0, last - 1]
    give[1, 1] = bond[0, first]
    for d in (1, 2):
        for i in (0, planes - 1):
            across(d, i)
        give[0, d + 1] = bond[d, last]
        give[1, d + 1] = bond[d, first]
    far = send_bonds(1, 1, 3, shared_rows(0))
    give[0, 0] = (2.0 / SCALE) * (coup[0, planes - 1] * mask[planes - 1])
    give[1, 0] = mask[0]
    near = send_bonds(0, 0, 1, own_half)
    send_middle(0)
    for d in (1, 2):
        for i in range(1, planes - 1):
            across(d, i)

    def strength(d, j):
        if d == 0 and j == 0:
            return got[0, 1]
        if d == 0 and j == high:
            return got[1, 1]
        if d > 0 and j == 1:
            return got[0, d + 1]
        if d > 0 and j == high:
            return got[1, d + 1]
        return bond[d, j]

    def factor(k):
        return 1.0 if k == 0 else 2.0

    def step(k, j):
        here = v[k, j]
        d0 = here - v[k, j + 1]
        d1 = here - following(here, 0)
        d2 = here - following(here, 1)
        f1 = strength(1, j) * d1
        f2 = strength(2, j) * d2
        inside = (f1 - preceding(f1, 0)) + (f2 - preceding(f2, 1))
        inside = inside + strength(0, j) * d0
        inside = inside + strength(0, j - 1) * (here - v[k, j - 1])
        if k == 0:
            v[1, j] = 0.5 * inside - here
        else:
            v[k + 1, j] = inside - 2.0 * here - v[k - 1, j]
        if first <= j <= last and k < STEPS - 1:
            du[0, k, j - first] = factor(k) * d0
            du[1, k, j - first] = factor(k) * d1
            du[2, k, j - first] = factor(k) * d2

    def moment(n, i, j):
        acc = v[i, first] * v[j, first]
        for plane in range(first + 1, last + 1):
            acc = acc + v[i, plane] * v[j, plane]
        row = jnp.sum(acc, axis=0, keepdims=True)
        part = row[:, :LANES]
        for start in range(LANES, row.shape[1], LANES):
            part = part + row[:, start:start + LANES]
        mom_a[p, pl.ds(n, 1), :] = part

    def product(n, d, i):
        acc = None
        for a in range(n // 2 + 1):
            term = du[d, a, i] * du[d, n - a, i]
            if a != n - a:
                term = 2.0 * term
            acc = term if acc is None else acc + term
        return acc

    def place(d, i):
        if d == 0:
            return 2 * planes + i
        return (d - 1) * planes + i

    every = [(d, i) for d in (1, 2, 0) for i in range(planes)]
    early = 3 * planes - 1

    def products(n):
        for d, i in every:
            q[n, place(d, i)] = product(n, d, i)

    def gradient_before(d, i, sums):
        acc = sums[1] * q[0, place(d, i)]
        for n in range(1, STEPS - 2):
            acc = acc + sums[n + 1] * q[n, place(d, i)]
        g[place(d, i)] = acc

    def gradient(d, i, sums):
        acc = g[place(d, i)]
        for n in (STEPS - 2, STEPS - 1):
            acc = acc + sums[n + 1] * product(n, d, i)
        g[place(d, i)] = pair[d, i] * acc

    def rows_of(index):
        return pl.ds(pl.multiple_of(index * block, block), block)

    parts = ((0, early // 2), (early // 2, early))
    rs_copies = {}

    def rs_start(level, part):
        bit = 1 << level
        other = flipped(p, bit)
        start, stop = parts[part]
        rs_copies[level, part] = []
        for j in range(probes // (2 * bit)):
            index = lax.rem(other, 2 * bit) + j * 2 * bit
            rs_copies[level, part].append(send(
                g.at[pl.ds(start, stop - start), rows_of(index)],
                recv.at[level, j, pl.ds(start, stop - start)],
                rs_send.at[level, j, part], rs_recv.at[level, j, part], {"probe": other},
            ))

    def rs_finish(level, part):
        bit = 1 << level
        start, stop = parts[part]
        here = pl.ds(start, stop - start)
        for j, copy in enumerate(rs_copies[level, part]):
            copy.wait_recv()
            index = lax.rem(p, 2 * bit) + j * 2 * bit
            g[here, rows_of(index)] = g[here, rows_of(index)] + recv[level, j, here]

    step(0, middle)
    send_middle(1)
    far = pass_far(0, far)
    near = pass_bonds(0, 0, 1, own_half, twin, near)
    mom_a[p, pl.ds(8, 8), :] = jnp.zeros((8, LANES), jnp.float32)
    moment(0, 0, 0)
    for copy in near:
        copy.wait_recv()
    bond[0, 1] = got[0, 0] * mask[0]
    pair[0, planes - 1] = mask[planes - 1] * (1.0 / SCALE) * got[1, 0]
    bond[0, last] = 2.0 * coup[0, planes - 1] * pair[0, planes - 1]
    edge_low.wait_recv()
    step(0, first)
    edge_high.wait_recv()
    step(0, last)
    step(1, middle)
    send_middle(2)
    for level in range(1, levels):
        far = pass_far(level, far)
    moment(1, 0, 1)
    moment(2, 1, 1)
    products(0)
    for copy in far:
        copy.wait_recv()

    a_copies, b_copies = [], []
    weights, sums = None, None
    for t in range(STEPS - 2):
        low_mid[t].wait_recv()
        step(t, 1)
        step(t + 1, first)
        high_mid[t].wait_recv()
        step(t, high)
        step(t + 1, last)
        if t == 2:
            moment(7, 3, 4)
            moment(8, 4, 4)
            for off in range(1, probes):
                a_copies.append(send(
                    mom_a.at[p], mom_a.at[p], ma_send.at[off], ma_recv.at[off],
                    {"probe": lax.rem(p + off, probes)},
                ))
        if t + 2 < STEPS - 1:
            step(t + 2, middle)
        if t + 3 < STEPS - 1:
            send_middle(t + 3)

        if t < 2:
            moment(2 * t + 3, t + 1, t + 2)
            moment(2 * t + 4, t + 2, t + 2)
        if t < STEPS - 3:
            products(t + 1)
        if t == 2:
            for copy in a_copies:
                copy.wait_recv()
            acc = mom_a[0]
            for index in range(1, probes):
                acc = acc + mom_a[index]
            mom_b[s] = acc
            for off in range(1, spaces):
                b_copies.append(send(
                    mom_b.at[s], mom_b.at[s], mb_send.at[off], mb_recv.at[off],
                    {"space": lax.rem(s + off, spaces)},
                ))
        if t == STEPS - 3:
            for n in (3, 4, 5):
                loads[n].wait()
            for copy in b_copies:
                copy.wait_recv()
            acc = mom_b[0]
            for index in range(1, spaces):
                acc = acc + mom_b[index]
            raw = jnp.sum(acc, axis=1, keepdims=True) / total_sites
            base = (raw[0:1], raw[1:2])
            moments = list(base)
            for n in range(2, STEPS + 1):
                moments.append(2.0 * raw[n:n + 1] - base[n % 2])
            points = target.shape[1]
            spectrum = jnp.zeros((1, points), jnp.float32)
            for n in range(STEPS + 1):
                spectrum = spectrum + scaled[n:n + 1, 0:1] * moments[n] * table[n:n + 1, :]
            misfit = spectrum - target[...]
            weights = []
            for n in range(STEPS + 1):
                dot = jnp.sum(table[n:n + 1, :] * misfit, axis=1, keepdims=True)
                weights.append((2.0 / points) * scaled[n:n + 1, 0:1] * dot)
            sums = [None] * (STEPS + 1)
            for n in range(STEPS, 0, -1):
                sums[n] = weights[n] if n + 2 > STEPS else weights[n] + sums[n + 2]
            for d, i in every:
                gradient_before(d, i, sums)
        if t == STEPS - 3:
            k = STEPS - 1
            for part, (start, stop) in enumerate(parts):
                for d, i in every[start:stop]:
                    here = v[k, first + i]
                    there = v[k, first + i + 1] if d == 0 else following(here, d - 1)
                    du[d, k, i] = 2.0 * (here - there)
                    gradient(d, i, sums)
                rs_start(0, part)
            step(t + 2, middle)
            for part in range(len(parts)):
                rs_finish(0, part)
                if levels > 1:
                    rs_start(1, part)
            for i in range(planes):
                acc = weights[0] * v[0, first + i]
                for n in range(1, STEPS):
                    acc = acc + weights[n] * v[n, first + i]
                costate[0, i] = 2.0 * acc

    k = STEPS - 1
    high_mid[k - 1].wait_recv()
    step(k - 1, high)
    du[0, k, planes - 1] = 2.0 * (v[k, last] - v[k, high])
    gradient(0, planes - 1, sums)
    d_copies = []
    for off in range(1, probes):
        other = lax.rem(p + off, probes)
        d_copies.append(send(
            g.at[early, rows_of(other)], direct.at[off - 1], d_send.at[off], d_recv.at[off],
            {"probe": other},
        ))
    step(k, last)
    low_mid[k - 1].wait_recv()
    step(k - 1, 1)
    step(k, first)
    for i in range(planes):
        costate[0, i] = costate[0, i] + 2.0 * weights[STEPS] * v[STEPS, first + i]
    for level in range(1, levels):
        for part in range(len(parts)):
            rs_finish(level, part)
            if level + 1 < levels:
                rs_start(level + 1, part)
    for d, i in every[:-1]:
        grad[d, i] = g[place(d, i), rows_of(p)]
    acc = g[early, rows_of(p)]
    for off in range(1, probes):
        d_copies[off - 1].wait_recv()
        acc = acc + direct[off - 1]
    grad[0, planes - 1] = acc
    for copy in started:
        copy.wait_send()


def on_device(probe_amplitudes, site_mask, couplings, target):
    spaces, probes = lax.axis_size("space"), lax.axis_size("probe")
    planes, rows, lanes = site_mask.shape
    table, scaled = tables(target.shape[0])
    block = rows // probes
    levels = probes.bit_length() - 1
    f32 = jnp.float32
    total_sites = float(probes * spaces * planes * rows * lanes)
    dma = pltpu.SemaphoreType.DMA
    costate, grad = pl.pallas_call(
        functools.partial(kernel, spaces, probes, total_sites),
        out_shape=(
            pltpu.VMEM((1, planes, rows, lanes), f32),
            pltpu.VMEM((3, planes, block, lanes), f32),
        ),
        in_specs=[pl.BlockSpec(memory_space=pltpu.HBM)] * 6,
        out_specs=(pl.BlockSpec(memory_space=pltpu.VMEM),) * 2,
        scratch_shapes=[
            pltpu.VMEM(probe_amplitudes.shape, f32),
            pltpu.VMEM(site_mask.shape, f32),
            pltpu.VMEM(couplings.shape, f32),
            pltpu.VMEM((1, target.shape[0]), f32),
            pltpu.VMEM(table.shape, f32),
            pltpu.VMEM(scaled.shape, f32),
            pltpu.VMEM((STEPS + 1, planes + 4, rows, lanes), f32),
            pltpu.VMEM((3, STEPS, planes, rows, lanes), f32),
            pltpu.VMEM((STEPS, 3 * planes, rows, lanes), f32),
            pltpu.VMEM((3 * planes, rows, lanes), f32),
            pltpu.VMEM((3, planes + 3, rows, lanes), f32),
            pltpu.VMEM((3, planes, rows, lanes), f32),
            pltpu.VMEM((2, 4, rows, lanes), f32),
            pltpu.VMEM((2, 4, rows, lanes), f32),
            pltpu.VMEM((probes, ROWS, LANES), f32),
            pltpu.VMEM((spaces, ROWS, LANES), f32),
            pltpu.VMEM((levels, probes // 2, 3 * planes - 1, block, lanes), f32),
            pltpu.VMEM((probes - 1, block, lanes), f32),
            dma((6,)), dma((2,)), dma((2,)), dma((STEPS, 2)), dma((STEPS, 2)),
            dma((2, 2)), dma((2, 2)), dma((1 + levels, 2)), dma((1 + levels, 2)),
            dma((probes,)), dma((probes,)), dma((spaces,)), dma((spaces,)),
            dma((levels, probes // 2, 2)), dma((levels, probes // 2, 2)),
            dma((probes,)), dma((probes,)),
        ],
        compiler_params=pltpu.CompilerParams(
            collective_id=0, has_side_effects=True, vmem_limit_bytes=63 * 1024 * 1024
        ),
    )(probe_amplitudes, site_mask, couplings, target[None], table, scaled)
    return costate, grad


def solution(mesh):
    return jax.shard_map(
        on_device,
        mesh=mesh,
        in_specs=(
            P(("groups", "probe"), "space", None, None),
            P(("groups", "space"), None, None),
            P(None, ("groups", "space"), None, None),
            P("groups"),
        ),
        out_specs=(
            P(("groups", "probe"), "space", None, None),
            P(None, ("groups", "space"), "probe", None),
        ),
        check_vma=False,
    )
```
